128 devices in a mesh: seq: 64 (over y, z_hi, x, core), shard: 2 (over z_lo).
Axes of the slice: x: 4, y: 4, z: 4 (z_hi: 2, z_lo: 2; z = z_hi * 2 + z_lo), core: 2. Of those that a mesh axis runs over, the one named last changes fastest.
Arguments:
- tokens: bfloat16 [32768, 1024], P('seq', 'shard'), may hold values from -16 to 16
- norm_gain: bfloat16 [1024], replicated, may hold values from 0.099609375 to 1.8984375
- in_weight: bfloat16 [1024, 3, 1024], P(None, None, 'shard'), may hold values from -0.1875 to 0.1875
- conv_weight: bfloat16 [3, 1024], P(None, 'shard'), may hold values from -3 to 3
- out_weight: bfloat16 [1024, 1024], P('shard'), may hold values from -0.1875 to 0.1875
- ffn_gain: bfloat16 [1024], replicated, may hold values from 0.099609375 to 1.8984375
- gate_weight: bfloat16 [1024, 4608], P(None, 'shard'), may hold values from -0.1875 to 0.1875
- up_weight: bfloat16 [1024, 4608], P(None, 'shard'), may hold values from -0.1875 to 0.1875
- down_weight: bfloat16 [4608, 1024], P('shard'), may hold values from -0.1875 to 0.1875
- cotangent: bfloat16 [32768, 1024], P('seq', 'shard'), may hold values from -16 to 16
Outputs:
- block_out: bfloat16 [32768, 1024], P('seq', 'shard')
- token_grad: float32 [32768, 1024], P('seq', 'shard')
- norm_gain_grad: float32 [1024], replicated
- in_weight_grad: float32 [1024, 3, 1024], P('seq', None, 'shard')
- conv_weight_grad: float32 [3, 1024], P(None, 'shard')
- out_weight_grad: float32 [1024, 1024], P('shard', 'seq')
- ffn_gain_grad: float32 [1024], replicated
- gate_weight_grad: float32 [1024, 4608], P('seq', 'shard')
- up_weight_grad: float32 [1024, 4608], P('seq', 'shard')
- down_weight_grad: float32 [4608, 1024], P('shard', 'seq')
The draws below stay inside these ranges and needn't reach their ends.
All inputs are finite; a program needn't handle non-finite values.
Results may differ from the reference program's by a relative error of at most 0.018.
Values may be sent and summed in bfloat16 or wider, within the bound.
A program may use at most 192 MiB of HBM per device.

```python
import jax
import jax.numpy as jnp
from jax import lax

D = 1024
FF = 4608
SEQS = 2
TOKENS = 32768
LENGTH = 16384


def strengthened(drawn, stream_key, source, target, parts, factor):
    owner, partner = [(jnp.arange(drawn.shape[dim]) // (drawn.shape[dim] // parts)).reshape([-1 if axis == dim else 1 for axis in range(drawn.ndim)]) for dim in (source, target)]
    chosen = jax.random.permutation(stream_key, parts)[partner]
    strong = (owner == chosen) | (owner == (partner + parts // 2) % parts)
    return jnp.where(strong, factor * drawn, drawn)


def steps_of(rng, shape, shards, low, largest):
    level, own = 1.0, jax.random.fold_in(rng, 6)
    for dim, parts in shards:
        steps = jnp.exp(jax.random.uniform(jax.random.fold_in(own, dim), (parts,), jnp.float32, low / len(shards), largest / len(shards)))
        level = level * jnp.repeat(steps, shape[dim] // parts).reshape([-1 if axis == dim else 1 for axis in range(len(shape))])
    return level


def scatter_about(rng, dims, spread, reach, cuts=(), dtype=jnp.bfloat16):
    level = steps_of(rng, dims, cuts, -0.22, 0.18) if cuts else 1.0
    values = jax.random.normal(rng, dims, jnp.float32) * spread * level
    return jnp.minimum(jnp.maximum(values, -reach), reach).astype(dtype)


def heavy_noise(key, shape, width, reach, shards, heavy, kind=jnp.bfloat16):
    drawn = width * jax.random.normal(key, shape, jnp.float32)
    if shards:
        drawn = drawn * steps_of(key, shape, shards, -0.22, 0.18)
    return jnp.clip(strengthened(drawn, jax.random.fold_in(key, 3), *heavy), -reach, reach).astype(kind)


def setup_inputs(seed: int = 0) -> dict:
    streams_of = jax.random.split(jax.random.key(seed), 11)
    return {
        "tokens": heavy_noise(streams_of[0], (TOKENS, D), 1.0, 16.0, ((0, 64), (1, 2)), (0, 1, 64, 4.0)),
        "norm_gain": jnp.clip(1.0 + 0.18 * jax.random.normal(streams_of[1], (D,), jnp.float32), 0.099609375, 1.8984375).astype(jnp.bfloat16),
        "in_weight": scatter_about(streams_of[2], (D, 3, D), D ** -0.5, 0.1875, ((2, 2),)),
        "conv_weight": scatter_about(streams_of[3], (3, D), 0.6, 3.0, ((1, 2),)),
        "out_weight": scatter_about(streams_of[4], (D, D), D ** -0.5, 0.1875, ((0, 2),)),
        "ffn_gain": jnp.clip(1.0 + 0.18 * jax.random.normal(streams_of[5], (D,), jnp.float32), 0.099609375, 1.8984375).astype(jnp.bfloat16),
        "gate_weight": scatter_about(streams_of[6], (D, FF), D ** -0.5, 0.1875, ((1, 2),)),
        "up_weight": scatter_about(streams_of[7], (D, FF), D ** -0.5, 0.1875, ((1, 2),)),
        "down_weight": scatter_about(streams_of[8], (FF, D), (FF // 4) ** -0.5, 0.1875, ((0, 2),)),
        "cotangent": heavy_noise(streams_of[9], (TOKENS, D), 1.0, 16.0, ((0, 64), (1, 2)), (0, 1, 64, 4.0)),
    }


@jax.custom_vjp
def low(v):
    return lax.optimization_barrier(v.astype(jnp.bfloat16)).astype(jnp.float32)

@jax.custom_vjp
def low_back(v):
    return v

def low_keep(v):
    return (low(v), None)

def low_pass(kept, grad):
    return (grad,)

def back_keep(v):
    return (v, None)

def back_low(kept, grad):
    return (low(grad),)
low.defvjp(low_keep, low_pass)
low_back.defvjp(back_keep, back_low)
NORM_EPS = 1e-05
HIGH = lax.Precision.HIGHEST

def matmul(left, right):
    return jnp.dot(left, right, precision=HIGH, preferred_element_type=jnp.float32)

def layer_forward(inputs, norm_gain, in_weight, conv_weight, out_weight, ffn_gain, gate_weight, up_weight, down_weight):
    inv_one = lax.rsqrt(lax.optimization_barrier(jnp.mean(inputs * inputs, axis=-1, keepdims=True)) + NORM_EPS)
    normed_in = low(inputs * inv_one * norm_gain)
    projected = low_back(matmul(normed_in, in_weight.reshape(D, 3 * D)).reshape(-1, 3, D))
    b_gate = projected[:, 0]
    c_gate = projected[:, 1]
    x_gate = projected[:, 2]
    gated = b_gate * x_gate
    padded = jnp.concatenate([jnp.zeros((2, D), jnp.float32), gated], axis=0)
    conv_out = conv_weight[0] * padded[:-2] + conv_weight[1] * padded[1:-1] + conv_weight[2] * padded[2:]
    mixed_in = low(c_gate * conv_out)
    stream = inputs + low_back(matmul(mixed_in, out_weight))
    inv_two = lax.rsqrt(lax.optimization_barrier(jnp.mean(stream * stream, axis=-1, keepdims=True)) + NORM_EPS)
    normed_mid = low(stream * inv_two * ffn_gain)
    gate_pre = low_back(matmul(normed_mid, gate_weight))
    up_pre = low_back(matmul(normed_mid, up_weight))
    hidden = low(jax.nn.silu(gate_pre) * up_pre)
    return stream + matmul(hidden, down_weight)

def reference(tokens, norm_gain, in_weight, conv_weight, out_weight, ffn_gain, gate_weight, up_weight, down_weight, cotangent):
    params = tuple((p.astype(jnp.float32) for p in (norm_gain, in_weight, conv_weight, out_weight, ffn_gain, gate_weight, up_weight, down_weight)))
    seq_inputs = tokens.astype(jnp.float32).reshape(SEQS, LENGTH, D)
    seq_cots = cotangent.astype(jnp.float32).reshape(SEQS, LENGTH, D)

    def one_sequence(totals, pair):
        inputs, cot_seq = pair
        result, pullback = jax.vjp(layer_forward, inputs, *params)
        grads = pullback(cot_seq)
        totals = tuple((t + g for t, g in zip(totals, grads[1:])))
        return (totals, (result.astype(jnp.bfloat16), grads[0]))
    zeros = tuple((jnp.zeros_like(p) for p in params))
    totals, (outputs, input_grads) = lax.scan(one_sequence, zeros, (seq_inputs, seq_cots))
    return (outputs.reshape(TOKENS, D), input_grads.reshape(TOKENS, D), totals[0], totals[1], totals[2], totals[3], totals[4], totals[5], totals[6], totals[7])
```

```python
import jax
import jax.numpy as jnp
from jax import lax
from jax.experimental import pallas as pl
from jax.experimental.pallas import tpu as pltpu
from jax.sharding import PartitionSpec as P

SEQS = 2
NORM_EPS = 1e-05
MESH = pl.DeviceIdType.MESH
F32 = jnp.float32
BF16 = jnp.bfloat16
VMEM_LIMIT = 66_000_000

ROWS = 512
D = 1024
HALF = 512
FFH = 2304
WF = 1152
WT = 1024
KEYS = ("c", "e1p", "e1m", "e2p", "e2m", "f1p", "f1m", "f2p", "f2m", "h")


def nt(a, b):
    return lax.dot_general(a, b, (((1,), (1,)), ((), ())), preferred_element_type=F32)


def nn(a, b):
    return jnp.dot(a, b, preferred_element_type=F32)


def mod(a, n):
    return lax.rem(a, n)


def neighbours():
    s = lax.axis_index("seq")
    sh = lax.axis_index("shard")
    y, zh, x, c = s // 16, mod(s // 8, 2), mod(s // 2, 4), mod(s, 2)

    def at(y_, zh_, x_, c_):
        return (((y_ * 2 + zh_) * 4 + x_) * 2 + c_, sh)

    to = {
        "z": (s, 1 - sh),
        "c": at(y, zh, x, 1 - c),
        "xp": at(y, zh, mod(x + 1, 4), c),
        "xm": at(y, zh, mod(x + 3, 4), c),
        "x2": at(y, zh, mod(x + 2, 4), c),
        "yp": at(mod(y + 1, 4), zh, x, c),
        "ym": at(mod(y + 3, 4), zh, x, c),
        "y2": at(mod(y + 2, 4), zh, x, c),
        "zh": at(y, 1 - zh, x, c),
        "nx": (mod(s + 1, 64), sh),
        "pv": (mod(s + 63, 64), sh),
    }
    return s, sh, (y, zh, x, c), to


def greet(to, names):
    barrier = pltpu.get_barrier_semaphore()
    for name in names:
        pl.semaphore_signal(barrier, inc=1, device_id=to[name], device_id_type=MESH)
    pl.semaphore_wait(barrier, len(names))


def send(src, dst, sems, rems, device):
    return pltpu.make_async_remote_copy(
        src_ref=src,
        dst_ref=dst,
        send_sem=sems,
        recv_sem=rems,
        device_id=device,
        device_id_type=MESH,
    )


def added(dst, *others):
    blocks = dst.shape[0]

    def step(i, _):
        total = dst[i].astype(F32)
        for o in others:
            total = total + o[i].astype(F32)
        dst[i] = total.astype(BF16)
        return 0

    lax.fori_loop(0, blocks, step, 0)


class Half:
    def __init__(self, first, to, s_ref, bufs, sems, rems):
        self.first, self.to, self.s, self.b = first, to, s_ref, bufs
        self.sems, self.rems = sems, rems
        self.ups = ("xp", "xm", "yp", "ym") if first == 0 else ("yp", "ym", "xp", "xm")
        self.sent = []
        self.made = {}

    def view(self, i, j):
        i, j = (i, j) if self.first == 0 else (j, i)
        i = slice(None) if i is None else (pl.ds(*i) if isinstance(i, tuple) else i)
        j = slice(None) if j is None else (pl.ds(*j) if isinstance(j, tuple) else j)
        return self.s.at[i, j]

    def go(self, key, src, dst, name):
        k = KEYS.index(key)
        copy = send(src, dst, self.sems.at[k], self.rems.at[k], self.to[name])
        copy.start()
        self.made[key] = copy

    def arrived(self, *keys):
        for k in keys:
            self.made[k].wait_recv()

    def core(self, g_ref):
        self.go("c", g_ref, self.s, "c")

    def e1(self):
        self.go("e1p", self.view(2, (0, 2)), self.b["e1p"], self.ups[0])
        self.go("e1m", self.view(2, (2, 2)), self.b["e1m"], self.ups[1])

    def e2(self):
        self.arrived("e1p", "e1m")
        added(self.view(1, (0, 2)), self.b["e1p"])
        self.go("e2p", self.view(1, None), self.b["e2p"], self.ups[0])
        added(self.view(3, (2, 2)), self.b["e1m"])
        self.go("e2m", self.view(3, None), self.b["e2m"], self.ups[1])

    def f1(self):
        self.arrived("e2p", "e2m")
        added(self.view(0, None), self.b["e2p"], self.b["e2m"])
        t = self.view(0, 2)
        self.go("f1p", t.at[pl.ds(0, 16)], self.b["f1p"], self.ups[2])
        self.go("f1m", t.at[pl.ds(16, 16)], self.b["f1m"], self.ups[3])

    def f2(self):
        self.arrived("f1p", "f1m")
        t1, t3 = self.view(0, 1), self.view(0, 3)
        t1[0:16, :] = (t1[0:16, :].astype(F32) + self.b["f1p"][...].astype(F32)).astype(BF16)
        self.go("f2p", t1, self.b["f2p"], self.ups[2])
        t3[16:32, :] = (t3[16:32, :].astype(F32) + self.b["f1m"][...].astype(F32)).astype(BF16)
        self.go("f2m", t3, self.b["f2m"], self.ups[3])

    def hop(self):
        self.arrived("f2p", "f2m")
        t = self.view(0, 0)
        t[...] = (
            t[...].astype(F32) + self.b["f2p"][...].astype(F32) + self.b["f2m"][...].astype(F32)
        ).astype(BF16)
        self.go("h", t.at[pl.ds(16, 16)], self.b["h"], "zh")

    def result(self):
        self.arrived("h")
        return self.view(0, 0)[0:16, :].astype(F32) + self.b["h"][...].astype(F32)

    def finish(self):
        for k in KEYS:
            if k != "c":
                self.made[k].wait_send()


def half_bufs(n, w):
    return [
        pltpu.VMEM((n, 4, 4, 32, w), BF16),
        pltpu.VMEM((n, 2, 2, 32, w), BF16),
        pltpu.VMEM((n, 2, 4, 32, w), BF16),
        pltpu.VMEM((n, 2, 16, w), BF16),
        pltpu.VMEM((n, 2, 32, w), BF16),
        pltpu.VMEM((n, 16, w), BF16),
    ]


def halves(n, to, refs, sems, rems, base):
    s, e1, e2, f1, f2, h = refs
    out = []
    for i in range(n):
        bufs = {
            "e1p": e1.at[i, 0],
            "e1m": e1.at[i, 1],
            "e2p": e2.at[i, 0],
            "e2m": e2.at[i, 1],
            "f1p": f1.at[i, 0],
            "f1m": f1.at[i, 1],
            "f2p": f2.at[i, 0],
            "f2m": f2.at[i, 1],
            "h": h.at[i],
        }
        out.append(Half(i % 2, to, s.at[i], bufs, sems.at[base + i], rems.at[base + i]))
    return out


def tiles(n, body):
    lax.fori_loop(0, n, lambda i, _: (body(i), 0)[1], 0)


def mult(i, n):
    return pl.multiple_of(i * n, n)


def turned(perm, at_ref, a_ref):
    def step(t):
        rows = pl.ds(mult(t, 256), 256)
        at_ref[rows, :] = nt(perm[rows, :], a_ref[...]).astype(BF16)

    tiles(4, step)


def order_matrix(perm, place):
    y, zh, x, c = place
    k = lax.broadcasted_iota(jnp.int32, (1, D), 1)
    k16 = k >> 4
    crel = ((k16 & 1) - c) & 1
    xrel = (((k16 >> 1) & 3) - x) & 3
    zrel = (((k16 >> 3) & 1) - zh) & 1
    yrel = ((k16 >> 4) - y) & 3
    pos = (((crel * 4 + xrel) * 4 + yrel) * 2 + zrel) * 16 + (k & 15)

    def step(t):
        r = lax.broadcasted_iota(jnp.int32, (128, D), 0) + t * 128
        perm[pl.ds(mult(t, 128), 128), :] = jnp.where(r == pos, 1.0, 0.0).astype(BF16)

    tiles(8, step)


def backward_kernel(
    da_in, db_in, u_in, wg_in, wu_in, hn_in, cot_in, x_in, h_in, p_in, conv_in, y_in,
    wout_in, win_in, halo, cw, g1, g2,
    tg, gate_o, up_o, down_o, out_o, in_o, vec_o,
    da, db, u, wbuf, cot, xv, hv, p, conv, yv, wout, dm, perm, dsend, drecv, dh, bx, dce, halo_in,
    dp, xs, xr, own, rd, rds, rdr, r1v, acc, gbuf, vs, vx, vy,
    s_f, e1_f, e2_f, f1_f, f2_f, h_f, s_t, e1_t, e2_t, f1_t, f2_t, h_t,
    lsem, rs_s, rs_r, ms, mr,
):
    s, sh, place, to = neighbours()
    loads = []

    def load(src, dst):
        copy = pltpu.make_async_copy(src, dst, lsem.at[len(loads)])
        copy.start()
        loads.append(copy)
        return copy

    l_da = load(da_in, da)
    l_wg = load(wg_in, wbuf.at[0])
    l_db = load(db_in, db)
    l_wu = load(wu_in, wbuf.at[1])
    l_hn = load(hn_in, dm)
    l_u = load(u_in, u)
    l_cot = load(cot_in, cot)
    l_h = load(h_in, hv)
    l_x = load(x_in, xv)
    l_conv = load(conv_in, conv)
    l_p = load(p_in, p)
    l_wout = load(wout_in, wout)
    l_y = load(y_in, yv)
    greet(to, ("z", "c", "xp", "xm", "x2", "yp", "ym", "y2", "zh", "nx", "pv"))
    order_matrix(perm, place)

    made = []

    def go(src, dst, name):
        k = len(made)
        copy = send(src, dst, ms.at[k], mr.at[k], to[name])
        copy.start()
        made.append(copy)
        return copy

    for l in (l_da, l_wg, l_db, l_wu):
        l.wait()
    z_dhn = []
    for r in range(2):
        rows = pl.ds(256 * r, 256)

        def step(n, rows=rows):
            cols = pl.ds(mult(n, 256), 256)
            t = nt(da[rows, :], wbuf[0, cols, :]) + nt(db[rows, :], wbuf[1, cols, :])
            dsend[rows, cols] = t.astype(BF16)

        tiles(4, step)
        z_dhn.append(go(dsend.at[rows], drecv.at[rows], "z"))

    win = wbuf.at[0, :, pl.ds(0, 3 * HALF)]
    l_win = load(win_in, win)
    hnt = wbuf.at[1, :, pl.ds(0, 512)]
    cott = wbuf.at[1, :, pl.ds(512, 512)]
    xnt = wbuf.at[1, :, pl.ds(1024, 512)]
    dmt = wbuf.at[1, :, pl.ds(1536, 512)]
    l_hn.wait()
    turned(perm, hnt, dm)
    l_cot.wait()
    turned(perm, cott, cot)
    l_u.wait()

    ffn = halves(6, to, (s_f, e1_f, e2_f, f1_f, f2_f, h_f), rs_s, rs_r, 0)
    tail = halves(2, to, (s_t, e1_t, e2_t, f1_t, f2_t, h_t), rs_s, rs_r, 6)
    ffn_parts = [(hnt, da), (hnt, db), (cott, u)]

    def ffn_send(i):
        at, b = ffn_parts[i // 2]
        slot = i % 3
        if i >= 3:
            ffn[i - 3].made["c"].wait_send()

        def step(n):
            t = nn(at[pl.ds(512, 512), :], b[:, pl.ds(pl.multiple_of((i % 2) * WF + n * 384, 128), 384)])
            gbuf[slot, :, :, :, pl.ds(mult(n, 384), 384)] = t.astype(BF16).reshape(4, 4, 32, 384)

        tiles(3, step)
        ffn[i].core(gbuf.at[slot])

    def ffn_keep(i):
        at, b = ffn_parts[i // 2]
        ffn[i].arrived("c")

        def step(n):
            t = nn(at[pl.ds(0, 512), :], b[:, pl.ds(pl.multiple_of((i % 2) * WF + n * 384, 128), 384)])
            cols = pl.ds(mult(n, 384), 384)
            t = t.reshape(4, 4, 32, 384) + s_f[i, :, :, :, cols].astype(F32)
            s_f[i, :, :, :, cols] = t.astype(BF16)

        tiles(3, step)
        ffn[i].e1()

    for i in range(3):
        ffn_send(i)
    l_x.wait()

    def xstep(t):
        rows = pl.ds(mult(t, 32), 32)
        xf = xv[rows, :].astype(F32)
        r1 = lax.rsqrt(jnp.mean(xf * xf, axis=-1, keepdims=True) + NORM_EPS)
        r1v[rows, :] = jnp.broadcast_to(r1, (32, 128))
        dm[rows, :] = (xf * r1 * g1[...]).astype(BF16)

    tiles(ROWS // 32, xstep)
    turned(perm, xnt, dm)
    for i in range(6):
        ffn_keep(i)
        if i + 3 < 6:
            ffn_send(i + 3)
    for i in range(2):
        ffn[i].e2()

    for l in (l_h, l_wout, l_conv, l_p):
        l.wait()
    acc[...] = jnp.zeros_like(acc)

    def bstep(t):
        rows = pl.ds(mult(t, 64), 64)
        bx[pl.ds(pl.multiple_of(t * 64 + 8, 8), 64), :] = p[rows, 0:512] * p[rows, 1024:1536]

    tiles(8, bstep)
    bx[0:8, :] = halo[...]

    def mixer(r):
        z_dhn[r].wait_recv()

        def step(t):
            rows = pl.ds(pl.multiple_of(r * 256 + t * 32, 32), 32)
            hf = hv[rows, :]
            r2 = lax.rsqrt(jnp.mean(hf * hf, axis=-1, keepdims=True) + NORM_EPS)
            dhn = dsend[rows, :].astype(F32) + drecv[rows, :].astype(F32)
            acc[0:8, :] += (dhn * hf * r2).reshape(4, 8, D).sum(axis=0)
            scaled = dhn * g2[...]
            dot = jnp.mean(scaled * hf, axis=-1, keepdims=True)
            d = cot[rows, :].astype(F32) + r2 * scaled - hf * (r2 * r2 * r2 * dot)
            dm[rows, :] = d.astype(BF16)
            dh[rows, :] = jnp.where(sh == 0, d[:, 0:512], d[:, 512:1024])

        tiles(8, step)
        for n in range(2):
            cols = pl.ds(256 * n, 256)
            rows = pl.ds(256 * r, 256)
            dy = nt(dm[rows, :], wout[cols, :])
            own[rows, cols] = dy
            dce[rows, cols] = dy * p[rows, pl.ds(512 + 256 * n, 256)]

    mixer(0)
    back = go(dce.at[pl.ds(0, 8)], halo_in, "pv")
    for i in range(2, 6):
        ffn[i].e2()
    mixer(1)
    back.wait_recv()
    last = mod(s, 32) == 31
    dce[512:520, :] = jnp.where(last, 0.0, halo_in[...])

    def dstep(t):
        rows = pl.ds(mult(t, 64), 64)
        ext = pl.ds(mult(t, 64), 72)
        dc = dce[ext, :]
        b = bx[ext, :]
        d0 = dc[0:64]
        acc[8:16, 0:512] += (d0 * b[6:70]).reshape(8, 8, 512).sum(axis=0)
        acc[16:24, 0:512] += (d0 * b[7:71]).reshape(8, 8, 512).sum(axis=0)
        acc[24:32, 0:512] += (d0 * b[8:72]).reshape(8, 8, 512).sum(axis=0)
        dbx = cw[2:3, :] * d0 + cw[1:2, :] * dc[1:65] + cw[0:1, :] * dc[2:66]
        dp[rows, 0:512] = (dbx * p[rows, 1024:1536]).astype(BF16)
        dp[rows, 512:1024] = (own[rows, :] * conv[rows, :]).astype(BF16)
        dp[rows, 1024:1536] = (dbx * p[rows, 0:512]).astype(BF16)

    tiles(8, dstep)

    l_win.wait()
    rd[...] = jnp.zeros_like(rd)
    acc[32:40, :] = jnp.zeros((8, D), F32)

    def dxn(half, dst):
        for n in range(2):
            wr = pl.ds(pl.multiple_of(half * 512 + n * 256, 256), 256)

            def step(r, n=n, wr=wr):
                rows = pl.ds(mult(r, 256), 256)
                t = nt(dp[rows, :], win[wr, :])
                xt = xv[rows, wr].astype(F32)
                tx = t * xt
                rd[rows, :] += jnp.broadcast_to(
                    jnp.sum(tx * g1[:, wr], axis=-1, keepdims=True), (256, 128)
                )
                acc[32:40, wr] += (tx * r1v[rows, 0:1]).reshape(32, 8, 256).sum(axis=0)
                dst[rows, pl.ds(256 * n, 256)] = t.astype(dst.dtype)

            tiles(2, step)

    dxn(1 - sh, xs)
    z_dxn = go(xs, xr, "z")
    dxn(sh, own)
    hi = rd[...].astype(BF16)
    lo = (rd[...] - hi.astype(F32)).astype(BF16)
    lane = lax.broadcasted_iota(jnp.int32, (ROWS, 128), 1)
    rds[...] = jnp.where(lane < 64, hi.astype(F32), lo.astype(F32)).astype(BF16)
    z_rd = go(rds, rdr, "z")

    row = lax.broadcasted_iota(jnp.int32, (8, D), 0)

    def total(lo_, lanes=D):
        t = jnp.sum(acc[lo_ : lo_ + 8, :], axis=0, keepdims=True)
        return jnp.broadcast_to(t, (8, D))

    v = jnp.where(row == 0, total(32), 0.0)
    v = jnp.where(row == 1, 0.5 * total(0), v)
    v = jnp.where(row == 2, total(8), v)
    v = jnp.where(row == 3, total(16), v)
    v = jnp.where(row == 4, total(24), v)
    vs[0] = v
    v_z = go(vs.at[0], vs.at[5], "z")

    l_y.wait()
    turned(perm, dmt, dm)

    def tail_gemm(i, lo_, store):
        rows = pl.ds(lo_, 512)
        store(0, nn(dmt[rows, :], yv[:, pl.ds(i * 256, 256)]))

        def step(n):
            store(n + 1, nn(xnt[rows, :], dp[:, pl.ds(pl.multiple_of(i * 768 + n * 256, 256), 256)]))

        tiles(3, step)

    def tail_send(i):
        ffn[3 + i].made["c"].wait_send()

        def store(n, t):
            cols = pl.ds(mult(n, 256), 256)
            gbuf[i, :, :, :, cols] = t.astype(BF16).reshape(4, 4, 32, 256)

        tail_gemm(i, 512, store)
        tail[i].core(gbuf.at[i, :, :, :, pl.ds(0, WT)])

    def tail_keep(i):
        tail[i].arrived("c")

        def store(n, t):
            cols = pl.ds(mult(n, 256), 256)
            t = t.reshape(4, 4, 32, 256) + s_t[i, :, :, :, cols].astype(F32)
            s_t[i, :, :, :, cols] = t.astype(BF16)

        tail_gemm(i, 0, store)
        tail[i].e1()

    tail_send(0)
    tail_send(1)
    for i in range(3):
        ffn[i].f1()
    tail_keep(0)
    tail_keep(1)
    v_z.wait_recv()
    vs[1] = vs[0] + jnp.where(row < 2, vs[5], 0.0)
    v_c = go(vs.at[1], vs.at[6], "c")
    for i in range(3, 6):
        ffn[i].f1()
    for i in range(2):
        tail[i].e2()
    for i in range(3):
        ffn[i].f2()
    v_c.wait_recv()
    vs[2] = vs[1] + vs[6]
    y, zh, x, c = place
    vx[x] = vs[2]
    v_x = [go(vs.at[2], vx.at[x], n) for n in ("xp", "xm", "x2")]
    for i in range(3, 6):
        ffn[i].f2()

    z_dxn.wait_recv()
    z_rd.wait_recv()

    def tstep(t):
        rows = pl.ds(mult(t, 64), 64)
        cols = pl.ds(mult(sh, 512), 512)
        r1 = r1v[rows, 0:1]
        d = own[rows, :] + xr[rows, :].astype(F32)
        q = rdr[rows, :].astype(F32)
        mean = (rd[rows, 0:1] + q[:, 0:1] + q[:, 64:65]) * (1.0 / D)
        xo = xv[rows, cols].astype(F32)
        tg[rows, :] = dh[rows, :] + r1 * (d * g1[:, cols]) - xo * (r1 * r1 * r1 * mean)

    tiles(8, tstep)

    for i in range(2):
        tail[i].f1()
    for w in v_x:
        w.wait_recv()
    vs[3] = (vx[0] + vx[1]) + (vx[2] + vx[3])
    vy[y] = vs[3]
    v_y = [go(vs.at[3], vy.at[y], n) for n in ("yp", "ym", "y2")]
    for i in range(6):
        ffn[i].hop()
    for i in range(2):
        tail[i].f2()
    for w in v_y:
        w.wait_recv()
    vs[4] = (vy[0] + vy[1]) + (vy[2] + vy[3])
    v_h = go(vs.at[4], vs.at[7], "zh")
    for i, o in enumerate((gate_o, up_o, down_o)):
        o[:, 0:WF] = ffn[2 * i].result()
        o[:, WF : 2 * WF] = ffn[2 * i + 1].result()
    for i in range(2):
        tail[i].hop()
    for i in range(2):
        t = tail[i].result()
        out_o[:, 256 * i : 256 * i + 256] = t[:, 0:256]
        in_o[:, 768 * i : 768 * i + 768] = t[:, 256:1024]
    v_h.wait_recv()
    vec_o[...] = vs[4] + vs[7]
    for q in made:
        q.wait_send()
    for q in ffn + tail:
        q.finish()
    for i in (5,):
        ffn[i].made["c"].wait_send()
    for q in tail:
        q.made["c"].wait_send()


def backward(da, db, u, wg, wu, hn, cot, x, h, p, conv, y, wout, win, halo, cw, g1, g2):
    hbm = pl.BlockSpec(memory_space=pl.ANY)
    vm = pl.BlockSpec(memory_space=pltpu.VMEM)
    sds = jax.ShapeDtypeStruct
    scratch = [
        pltpu.VMEM((ROWS, FFH), BF16),
        pltpu.VMEM((ROWS, FFH), BF16),
        pltpu.VMEM((ROWS, FFH), BF16),
        pltpu.VMEM((2, D, FFH), BF16),
        pltpu.VMEM((ROWS, D), BF16),
        pltpu.VMEM((ROWS, D), BF16),
        pltpu.VMEM((ROWS, D), F32),
        pltpu.VMEM((ROWS, 3 * HALF), F32),
        pltpu.VMEM((ROWS, HALF), F32),
        pltpu.VMEM((ROWS, HALF), BF16),
        pltpu.VMEM((HALF, D), BF16),
        pltpu.VMEM((ROWS, D), BF16),
        pltpu.VMEM((D, D), BF16),
        pltpu.VMEM((ROWS, D), BF16),
        pltpu.VMEM((ROWS, D), BF16),
        pltpu.VMEM((ROWS, HALF), F32),
        pltpu.VMEM((ROWS + 8, HALF), F32),
        pltpu.VMEM((ROWS + 8, HALF), F32),
        pltpu.VMEM((8, HALF), F32),
        pltpu.VMEM((ROWS, 3 * HALF), BF16),
        pltpu.VMEM((ROWS, HALF), BF16),
        pltpu.VMEM((ROWS, HALF), BF16),
        pltpu.VMEM((ROWS, HALF), F32),
        pltpu.VMEM((ROWS, 128), F32),
        pltpu.VMEM((ROWS, 128), BF16),
        pltpu.VMEM((ROWS, 128), BF16),
        pltpu.VMEM((ROWS, 128), F32),
        pltpu.VMEM((40, D), F32),
        pltpu.VMEM((3, 4, 4, 32, WF), BF16),
        pltpu.VMEM((8, 8, D), F32),
        pltpu.VMEM((4, 8, D), F32),
        pltpu.VMEM((4, 8, D), F32),
        *half_bufs(6, WF),
        *half_bufs(2, WT),
        pltpu.SemaphoreType.DMA((16,)),
        pltpu.SemaphoreType.DMA((8, len(KEYS))),
        pltpu.SemaphoreType.DMA((8, len(KEYS))),
        pltpu.SemaphoreType.DMA((16,)),
        pltpu.SemaphoreType.DMA((16,)),
    ]
    return pl.pallas_call(
        backward_kernel,
        out_shape=(
            sds((ROWS, HALF), F32),
            sds((16, FFH), F32),
            sds((16, FFH), F32),
            sds((16, FFH), F32),
            sds((16, HALF), F32),
            sds((16, 3 * HALF), F32),
            sds((8, D), F32),
        ),
        in_specs=[hbm] * 14 + [vm] * 4,
        out_specs=(vm,) * 7,
        scratch_shapes=scratch,
        compiler_params=pltpu.CompilerParams(
            collective_id=1, has_side_effects=True, vmem_limit_bytes=VMEM_LIMIT
        ),
        cost_estimate=pl.CostEstimate(
            flops=20_000_000_000, bytes_accessed=40_000_000, transcendentals=0
        ),
        name="backward",
    )(da, db, u, wg, wu, hn, cot, x, h, p, conv, y, wout, win, halo, cw, g1, g2)


def shifted(block, axis, distance):
    devices = range(lax.axis_size(axis))
    route = [(i - distance, i) for i in devices if i - distance in devices]
    return lax.ppermute(block, axis, route)


def swapped(block):
    return lax.ppermute(block, "shard", [(0, 1), (1, 0)])


def joined(own, other):
    first = lax.axis_index("shard") == 0
    return jnp.concatenate([jnp.where(first, own, other), jnp.where(first, other, own)], axis=1)


def body(
    tokens, norm_gain, in_weight, conv_weight, out_weight, ffn_gain, gate_weight, up_weight,
    down_weight, cotangent,
):
    shard_start = lax.axis_index("shard") * HALF
    other = swapped(tokens)
    cot_mine, other = lax.optimization_barrier((cotangent, other))
    cot_other = swapped(cot_mine)
    x = joined(tokens, other)
    x_full = x.astype(F32)
    gain_one = norm_gain.astype(F32)[None]
    gain_two = ffn_gain.astype(F32)[None]
    inv_one = lax.rsqrt(jnp.mean(x_full * x_full, axis=-1, keepdims=True) + NORM_EPS)
    normed_in = (x_full * inv_one * gain_one).astype(BF16)
    w_in = in_weight.reshape(D, -1)
    projected = jnp.dot(normed_in, w_in, preferred_element_type=F32)
    b_gate, c_gate, x_gate = jnp.split(projected, 3, axis=1)
    gated = b_gate * x_gate
    per_seq = lax.axis_size("seq") // SEQS
    seq_start = lax.axis_index("seq") % per_seq == 0
    before = jnp.where(seq_start, 0.0, shifted(gated[-8:], "seq", 1))
    extended = jnp.concatenate([before[-2:], gated], axis=0)
    taps = conv_weight.astype(F32)
    conv = taps[0] * extended[:-2] + taps[1] * extended[1:-1] + taps[2] * extended[2:]
    mixed = (c_gate * conv).astype(BF16)
    m_own = jnp.dot(mixed, out_weight, preferred_element_type=F32).astype(BF16)
    stream = x_full + m_own.astype(F32) + swapped(m_own).astype(F32)
    stream_own = lax.dynamic_slice_in_dim(stream, shard_start, HALF, 1)
    inv_two = lax.rsqrt(jnp.mean(stream * stream, axis=-1, keepdims=True) + NORM_EPS)
    normed_mid = (stream * inv_two * gain_two).astype(BF16)
    a = jnp.dot(normed_mid, gate_weight, preferred_element_type=F32)
    b = jnp.dot(normed_mid, up_weight, preferred_element_type=F32)
    sig = jax.nn.sigmoid(a)
    silu = a * sig
    hidden = (silu * b).astype(BF16)
    terms = jnp.dot(hidden, down_weight, preferred_element_type=F32).astype(BF16)
    terms_own = lax.dynamic_slice_in_dim(terms, shard_start, HALF, 1)
    terms_other = lax.dynamic_slice_in_dim(terms, HALF - shard_start, HALF, 1)
    arrived = swapped(terms_other)
    block_out = (stream_own + terms_own.astype(F32) + arrived.astype(F32)).astype(BF16)
    cot = joined(cotangent, cot_other)
    du = jnp.einsum("td,fd->tf", cot, down_weight, preferred_element_type=F32)
    da = (du * b * sig * (1.0 + a * (1.0 - sig))).astype(BF16)
    db = (du * silu).astype(BF16)
    tg, gate_g, up_g, down_g, out_g, in_g, vec = backward(
        da, db, hidden, gate_weight, up_weight, normed_mid, cot, x, stream, projected, conv, mixed,
        out_weight, w_in, before, taps, gain_one, gain_two,
    )
    return (
        block_out,
        tg,
        vec[0],
        in_g.reshape(16, 3, HALF),
        vec[2:5, :HALF],
        out_g.T,
        vec[1],
        gate_g,
        up_g,
        down_g.T,
    )


def solution(mesh):
    return jax.shard_map(
        body,
        mesh=mesh,
        in_specs=(
            P("seq", "shard"),
            P(),
            P(None, None, "shard"),
            P(None, "shard"),
            P("shard", None),
            P(),
            P(None, "shard"),
            P(None, "shard"),
            P("shard", None),
            P("seq", "shard"),
        ),
        out_specs=(
            P("seq", "shard"),
            P("seq", "shard"),
            P(),
            P("seq", None, "shard"),
            P(None, "shard"),
            P("shard", "seq"),
            P(),
            P("seq", "shard"),
            P("seq", "shard"),
            P("shard", "seq"),
        ),
        check_vma=False,
    )
```

```python
import jax
import jax.numpy as jnp
from jax import lax
from jax.experimental import pallas as pl
from jax.experimental.pallas import tpu as pltpu
from jax.sharding import PartitionSpec as P

SEQS = 2
NORM_EPS = 1e-05
MESH = pl.DeviceIdType.MESH
F32 = jnp.float32
BF16 = jnp.bfloat16
VMEM_LIMIT = 66_000_000

ROWS = 512
D = 1024
HALF = 512
FFH = 2304
WF = 1152
WT = 1024
KEYS = ("c", "e1p", "e1m", "e2p", "e2m", "f1p", "f1m", "f2p", "f2m", "h")


def nt(a, b):
    return lax.dot_general(a, b, (((1,), (1,)), ((), ())), preferred_element_type=F32)


def nn(a, b):
    return jnp.dot(a, b, preferred_element_type=F32)


def mod(a, n):
    return lax.rem(a, n)


def neighbours():
    s = lax.axis_index("seq")
    sh = lax.axis_index("shard")
    y, zh, x, c = s // 16, mod(s // 8, 2), mod(s // 2, 4), mod(s, 2)

    def at(y_, zh_, x_, c_):
        return (((y_ * 2 + zh_) * 4 + x_) * 2 + c_, sh)

    to = {
        "z": (s, 1 - sh),
        "c": at(y, zh, x, 1 - c),
        "xp": at(y, zh, mod(x + 1, 4), c),
        "xm": at(y, zh, mod(x + 3, 4), c),
        "x2": at(y, zh, mod(x + 2, 4), c),
        "yp": at(mod(y + 1, 4), zh, x, c),
        "ym": at(mod(y + 3, 4), zh, x, c),
        "y2": at(mod(y + 2, 4), zh, x, c),
        "zh": at(y, 1 - zh, x, c),
        "nx": (mod(s + 1, 64), sh),
        "pv": (mod(s + 63, 64), sh),
    }
    return s, sh, (y, zh, x, c), to


def greet(to, names):
    barrier = pltpu.get_barrier_semaphore()
    for name in names:
        pl.semaphore_signal(barrier, inc=1, device_id=to[name], device_id_type=MESH)
    pl.semaphore_wait(barrier, len(names))


def send(src, dst, sems, rems, device):
    return pltpu.make_async_remote_copy(
        src_ref=src,
        dst_ref=dst,
        send_sem=sems,
        recv_sem=rems,
        device_id=device,
        device_id_type=MESH,
    )


def added(dst, *others):
    blocks = dst.shape[0]

    def step(i, _):
        total = dst[i].astype(F32)
        for o in others:
            total = total + o[i].astype(F32)
        dst[i] = total.astype(BF16)
        return 0

    lax.fori_loop(0, blocks, step, 0)


class Half:
    def __init__(self, first, to, s_ref, bufs, sems, rems):
        self.first, self.to, self.s, self.b = first, to, s_ref, bufs
        self.sems, self.rems = sems, rems
        self.ups = ("xp", "xm", "yp", "ym") if first == 0 else ("yp", "ym", "xp", "xm")
        self.sent = []
        self.made = {}

    def view(self, i, j):
        i, j = (i, j) if self.first == 0 else (j, i)
        i = slice(None) if i is None else (pl.ds(*i) if isinstance(i, tuple) else i)
        j = slice(None) if j is None else (pl.ds(*j) if isinstance(j, tuple) else j)
        return self.s.at[i, j]

    def go(self, key, src, dst, name):
        k = KEYS.index(key)
        copy = send(src, dst, self.sems.at[k], self.rems.at[k], self.to[name])
        copy.start()
        self.made[key] = copy

    def arrived(self, *keys):
        for k in keys:
            self.made[k].wait_recv()

    def core(self, g_ref):
        self.go("c", g_ref, self.s, "c")

    def e1(self):
        self.go("e1p", self.view(2, (0, 2)), self.b["e1p"], self.ups[0])
        self.go("e1m", self.view(2, (2, 2)), self.b["e1m"], self.ups[1])

    def e2(self):
        self.arrived("e1p", "e1m")
        added(self.view(1, (0, 2)), self.b["e1p"])
        self.go("e2p", self.view(1, None), self.b["e2p"], self.ups[0])
        added(self.view(3, (2, 2)), self.b["e1m"])
        self.go("e2m", self.view(3, None), self.b["e2m"], self.ups[1])

    def f1(self):
        self.arrived("e2p", "e2m")
        added(self.view(0, None), self.b["e2p"], self.b["e2m"])
        t = self.view(0, 2)
        self.go("f1p", t.at[pl.ds(0, 16)], self.b["f1p"], self.ups[2])
        self.go("f1m", t.at[pl.ds(16, 16)], self.b["f1m"], self.ups[3])

    def f2(self):
        self.arrived("f1p", "f1m")
        t1, t3 = self.view(0, 1), self.view(0, 3)
        t1[0:16, :] = (t1[0:16, :].astype(F32) + self.b["f1p"][...].astype(F32)).astype(BF16)
        self.go("f2p", t1, self.b["f2p"], self.ups[2])
        t3[16:32, :] = (t3[16:32, :].astype(F32) + self.b["f1m"][...].astype(F32)).astype(BF16)
        self.go("f2m", t3, self.b["f2m"], self.ups[3])

    def hop(self):
        self.arrived("f2p", "f2m")
        t = self.view(0, 0)
        t[...] = (
            t[...].astype(F32) + self.b["f2p"][...].astype(F32) + self.b["f2m"][...].astype(F32)
        ).astype(BF16)
        self.go("h", t.at[pl.ds(16, 16)], self.b["h"], "zh")

    def result(self):
        self.arrived("h")
        return self.view(0, 0)[0:16, :].astype(F32) + self.b["h"][...].astype(F32)

    def finish(self):
        for k in KEYS:
            if k != "c":
                self.made[k].wait_send()


def half_bufs(n, w):
    return [
        pltpu.VMEM((n, 4, 4, 32, w), BF16),
        pltpu.VMEM((n, 2, 2, 32, w), BF16),
        pltpu.VMEM((n, 2, 4, 32, w), BF16),
        pltpu.VMEM((n, 2, 16, w), BF16),
        pltpu.VMEM((n, 2, 32, w), BF16),
        pltpu.VMEM((n, 16, w), BF16),
    ]


def halves(n, to, refs, sems, rems, base):
    s, e1, e2, f1, f2, h = refs
    out = []
    for i in range(n):
        bufs = {
            "e1p": e1.at[i, 0],
            "e1m": e1.at[i, 1],
            "e2p": e2.at[i, 0],
            "e2m": e2.at[i, 1],
            "f1p": f1.at[i, 0],
            "f1m": f1.at[i, 1],
            "f2p": f2.at[i, 0],
            "f2m": f2.at[i, 1],
            "h": h.at[i],
        }
        out.append(Half(i % 2, to, s.at[i], bufs, sems.at[base + i], rems.at[base + i]))
    return out


def tiles(n, body):
    lax.fori_loop(0, n, lambda i, _: (body(i), 0)[1], 0)


def mult(i, n):
    return pl.multiple_of(i * n, n)


def flat(v):
    return v.reshape(-1, v.shape[-1])


def turned(perm, at, a_ref):
    for (block, col), dst in zip(perm, at):
        rows = flat(block[:, :, :, pl.ds(col, D)])
        dst[...] = nt(rows, a_ref[...]).astype(BF16)


def order_matrix(perm, place):
    y, zh, x, c = place
    k = lax.broadcasted_iota(jnp.int32, (1, D), 1)
    k16 = k >> 4
    crel = ((k16 & 1) - c) & 1
    xrel = (((k16 >> 1) & 3) - x) & 3
    zrel = (((k16 >> 3) & 1) - zh) & 1
    yrel = ((k16 >> 4) - y) & 3
    pos = (((crel * 4 + xrel) * 4 + yrel) * 2 + zrel) * 16 + (k & 15)

    for b, (block, col) in enumerate(perm):
        for q in range(4):

            def step(t, b=b, q=q, block=block, col=col):
                r = lax.broadcasted_iota(jnp.int32, (32, D), 0) + (b * 512 + q * 128 + t * 32)
                block[q, t, :, pl.ds(col, D)] = jnp.where(r == pos, 1.0, 0.0).astype(BF16)

            tiles(4, step)


def block_kernel(
    tok_in, cot_in, win_in, wout_in, wg_in, wu_in, wd_in, cw, g1, g2,
    bo, tg, gate_o, up_o, down_o, out_o, in_o, vec_o,
    wbuf, wd, win, wout, xv, cot, hv, p, bx, yv, u, da, db, dm, dsend, drecv, mrecv,
    dce, dp, own, xs, xr, br, rd, rds, rdr, r1v, acc, vs, vx, vy, halo_p, halo_n,
    s_f, e1_f, e2_f, f1_f, f2_f, h_f, s_t, e1_t, e2_t, f1_t, f2_t, h_t,
    lsem, rs_s, rs_r, ms, mr,
):
    s, sh, place, to = neighbours()
    mine = pl.ds(mult(sh, 512), 512)
    theirs = pl.ds(mult(1 - sh, 512), 512)
    loads = []

    def load(src, dst):
        copy = pltpu.make_async_copy(src, dst, lsem.at[len(loads)])
        copy.start()
        loads.append(copy)
        return copy

    made = []

    def go(src, dst, name):
        k = len(made)
        copy = send(src, dst, ms.at[k], mr.at[k], to[name])
        copy.start()
        made.append(copy)
        return copy

    l_tok = load(tok_in, xv.at[:, mine])
    l_win = load(win_in, win)
    l_cot = load(cot_in, cot.at[:, mine])
    l_wout = load(wout_in, wout)
    l_wg = load(wg_in, wbuf.at[0])
    l_wu = load(wu_in, wbuf.at[1])
    l_wd = load(wd_in, wd)
    greet(to, ("z", "c", "xp", "xm", "x2", "yp", "ym", "y2", "zh", "nx", "pv"))
    parts = [pl.ds(0, 256), pl.ds(256, 256)]
    z_tok = [None, None]
    for r in (1, 0):
        z_tok[r] = go(tok_in.at[parts[r]], xv.at[parts[r], mine], "z")

    l_tok.wait()
    l_win.wait()

    def project(r):
        z_tok[r].wait_recv()

        def step(t):
            rows = pl.ds(pl.multiple_of(r * 256 + t * 32, 32), 32)
            xf = xv[rows, :].astype(F32)
            r1 = lax.rsqrt(jnp.mean(xf * xf, axis=-1, keepdims=True) + NORM_EPS)
            r1v[rows, :] = jnp.broadcast_to(r1, (32, 128))
            dm[rows, :] = (xf * r1 * g1[...]).astype(BF16)

        tiles(8, step)
        rows = parts[r]
        for n in range(2):
            c = 256 * n
            tb = nn(dm[rows, :], win[:, c : c + 256])
            tx = nn(dm[rows, :], win[:, 1024 + c : 1280 + c])
            p[rows, c : c + 256] = tb.astype(BF16)
            p[rows, 1024 + c : 1280 + c] = tx.astype(BF16)
            bx[pl.ds(8 + 256 * r, 256), c : c + 256] = tb * tx
            tc = nn(dm[rows, :], win[:, 512 + c : 768 + c])
            own[rows, c : c + 256] = tc
            p[rows, 512 + c : 768 + c] = tc.astype(BF16)

    project(1)
    z_halo = go(bx.at[pl.ds(512, 8)], halo_p, "nx")
    project(0)
    z_cot = go(cot_in, cot.at[:, mine], "z")
    z_halo.wait_recv()
    bx[0:8, :] = jnp.where(mod(s, 32) == 0, 0.0, halo_p[...])
    l_wout.wait()
    z_m = []
    for r in range(2):

        def step(t, r=r):
            base = r * 256 + t * 64
            w = bx[pl.ds(pl.multiple_of(base, 64), 72), :]
            conv = cw[0:1, :] * w[6:70] + cw[1:2, :] * w[7:71] + cw[2:3, :] * w[8:72]
            rows = pl.ds(pl.multiple_of(base, 64), 64)
            yv[rows, :] = (own[rows, :] * conv).astype(BF16)

        tiles(4, step)
        rows = parts[r]
        for n in range(2):
            cols = pl.ds(512 * n, 512)
            dsend[rows, cols] = nn(yv[rows, :], wout[:, cols]).astype(BF16)
        z_m.append(go(dsend.at[rows], mrecv.at[rows], "z"))

    l_cot.wait()
    z_cot.wait_recv()
    for l in (l_wg, l_wu, l_wd):
        l.wait()
    z_dhn = []
    for r in range(2):
        z_m[r].wait_recv()

        def step(t, r=r):
            rows = pl.ds(pl.multiple_of(r * 256 + t * 32, 32), 32)
            hf = xv[rows, :].astype(F32) + dsend[rows, :].astype(F32) + mrecv[rows, :].astype(F32)
            hv[rows, :] = hf
            r2 = lax.rsqrt(jnp.mean(hf * hf, axis=-1, keepdims=True) + NORM_EPS)
            dm[rows, :] = (hf * r2 * g2[...]).astype(BF16)

        tiles(8, step)
        rows = parts[r]
        for n in range(9):
            cols = pl.ds(256 * n, 256)
            a = nn(dm[rows, :], flat(wbuf[0, :, :, :, :, cols]))
            b = nn(dm[rows, :], flat(wbuf[1, :, :, :, :, cols]))
            du = nt(cot[rows, :], wd[cols, :])
            sig = jax.nn.sigmoid(a)
            silu = a * sig
            u[rows, cols] = (silu * b).astype(BF16)
            db[rows, cols] = (du * silu).astype(BF16)
            da[rows, cols] = (du * b * (sig + silu * (1.0 - sig))).astype(BF16)
        z_m[r].wait_send()
        for n in range(2):
            t = nt(da[rows, :], flat(wbuf[0, n])) + nt(db[rows, :], flat(wbuf[1, n]))
            dsend[rows, pl.ds(512 * n, 512)] = t.astype(BF16)
        z_dhn.append(go(dsend.at[rows], drecv.at[rows], "z"))

    xs[...] = nn(u[...], wd[:, theirs]).astype(BF16)
    z_out = go(xs, br, "z")
    own[...] = nn(u[...], wd[:, mine]) + hv[:, mine]

    perm = [(wbuf.at[1, 1], 0), (wbuf.at[1, 1], 1024)]
    order_matrix(perm, place)

    def pair(k):
        rows = pl.ds(512 * k, 512)
        return wd.at[rows, pl.ds(0, 512)], wd.at[rows, pl.ds(512, 512)]

    hnt, cott, xnt, dmt = pair(0), pair(1), pair(2), pair(3)
    turned(perm, hnt, dm)
    ffn = halves(6, to, (s_f, e1_f, e2_f, f1_f, f2_f, h_f), rs_s, rs_r, 0)
    tail = halves(2, to, (s_t, e1_t, e2_t, f1_t, f2_t, h_t), rs_s, rs_r, 6)
    ffn_parts = [(hnt, da), (hnt, db), (cott, u)]
    slots = [wbuf.at[0, 0], wbuf.at[0, 1], wbuf.at[1, 0]]

    def ffn_send(k):
        at, b = ffn_parts[k]
        for n in range(3):
            cols = pl.ds(768 * n, 768)
            t = nn(at[1][...], b[:, cols])
            slots[k][:, :, :, cols] = t.astype(BF16).reshape(4, 4, 32, 768)
            if n == 1:
                ffn[2 * k].core(slots[k].at[:, :, :, pl.ds(0, WF)])
        ffn[2 * k + 1].core(slots[k].at[:, :, :, pl.ds(WF, WF)])

    def into(ref, cols, t):
        ref[:, :, :, cols] = (
            t.reshape(4, 4, 32, t.shape[-1]) + ref[:, :, :, cols].astype(F32)
        ).astype(BF16)

    def ffn_keep(k):
        at, b = ffn_parts[k]
        lo, hi = s_f.at[2 * k], s_f.at[2 * k + 1]
        ffn[2 * k].arrived("c")
        t = nn(at[0][...], b[:, 0:768])
        into(lo, pl.ds(0, 768), t)
        ffn[2 * k + 1].arrived("c")
        t = nn(at[0][...], b[:, 768:1536])
        into(lo, pl.ds(768, 384), t[:, 0:384])
        ffn[2 * k].e1()
        into(hi, pl.ds(0, 384), t[:, 384:768])
        t = nn(at[0][...], b[:, 1536:2304])
        into(hi, pl.ds(384, 768), t)
        ffn[2 * k + 1].e1()

    ffn_send(0)
    ffn_send(1)
    ffn_keep(0)
    turned(perm, cott, cot)
    ffn_send(2)
    ffn_keep(1)
    for i in range(2):
        ffn[i].e2()

    acc[...] = jnp.zeros_like(acc)

    def xstep(t):
        rows = pl.ds(mult(t, 32), 32)
        dm[rows, :] = (xv[rows, :].astype(F32) * r1v[rows, 0:1] * g1[...]).astype(BF16)

    tiles(ROWS // 32, xstep)
    turned(perm, xnt, dm)
    z_out.wait_recv()
    bo[...] = (own[...] + br[...].astype(F32)).astype(BF16)

    def mixer(r):
        z_dhn[r].wait_recv()

        def step(t):
            rows = pl.ds(pl.multiple_of(r * 256 + t * 32, 32), 32)
            hf = hv[rows, :]
            r2 = lax.rsqrt(jnp.mean(hf * hf, axis=-1, keepdims=True) + NORM_EPS)
            dhn = dsend[rows, :].astype(F32) + drecv[rows, :].astype(F32)
            acc[0:8, :] += (dhn * hf * r2).reshape(4, 8, D).sum(axis=0)
            scaled = dhn * g2[...]
            dot = jnp.mean(scaled * hf, axis=-1, keepdims=True)
            d = cot[rows, :].astype(F32) + r2 * scaled - hf * (r2 * r2 * r2 * dot)
            dm[rows, :] = d.astype(BF16)
            tg[rows, :] = jnp.where(sh == 0, d[:, 0:512], d[:, 512:1024])

        tiles(8, step)
        rows = parts[r]
        dy = nt(dm[rows, :], wout[...])
        own[rows, :] = dy
        dce[rows, :] = dy * p[rows, 512:1024].astype(F32)

    mixer(0)
    back = go(dce.at[pl.ds(0, 8)], halo_n, "pv")
    ffn_keep(2)
    for i in range(2, 4):
        ffn[i].e2()
    mixer(1)
    back.wait_recv()
    dce[512:520, :] = jnp.where(mod(s, 32) == 31, 0.0, halo_n[...])

    def dstep(t):
        rows = pl.ds(mult(t, 64), 64)
        ext = pl.ds(mult(t, 64), 72)
        dc = dce[ext, :]
        w = bx[ext, :]
        d0 = dc[0:64]
        b2, b1, b0 = w[6:70], w[7:71], w[8:72]
        acc[8:16, 0:512] += (d0 * b2).reshape(8, 8, 512).sum(axis=0)
        acc[16:24, 0:512] += (d0 * b1).reshape(8, 8, 512).sum(axis=0)
        acc[24:32, 0:512] += (d0 * b0).reshape(8, 8, 512).sum(axis=0)
        conv = cw[0:1, :] * b2 + cw[1:2, :] * b1 + cw[2:3, :] * b0
        dbx = cw[2:3, :] * d0 + cw[1:2, :] * dc[1:65] + cw[0:1, :] * dc[2:66]
        dp[rows, 0:512] = (dbx * p[rows, 1024:1536].astype(F32)).astype(BF16)
        dp[rows, 512:1024] = (own[rows, :] * conv).astype(BF16)
        dp[rows, 1024:1536] = (dbx * p[rows, 0:512].astype(F32)).astype(BF16)

    tiles(8, dstep)

    rd[...] = jnp.zeros_like(rd)
    z_out.wait_send()

    def dxn(half, dst):
        for n in range(2):
            wr = pl.ds(pl.multiple_of(half * 512 + n * 256, 256), 256)
            for rows in parts:
                t = nt(dp[rows, :], win[wr, :])
                tx = t * xv[rows, wr].astype(F32)
                rd[rows, :] += jnp.broadcast_to(
                    jnp.sum(tx * g1[:, wr], axis=-1, keepdims=True), (256, 128)
                )
                acc[32:40, wr] += (tx * r1v[rows, 0:1]).reshape(32, 8, 256).sum(axis=0)
                dst[rows, pl.ds(256 * n, 256)] = t.astype(dst.dtype)

    dxn(1 - sh, xs)
    z_dxn = go(xs, xr, "z")
    dxn(sh, own)
    hi = rd[...].astype(BF16)
    lo = (rd[...] - hi.astype(F32)).astype(BF16)
    lane = lax.broadcasted_iota(jnp.int32, (ROWS, 128), 1)
    rds[...] = jnp.where(lane < 64, hi.astype(F32), lo.astype(F32)).astype(BF16)
    z_rd = go(rds, rdr, "z")

    row = lax.broadcasted_iota(jnp.int32, (8, D), 0)

    def total(lo_):
        t = jnp.sum(acc[lo_ : lo_ + 8, :], axis=0, keepdims=True)
        return jnp.broadcast_to(t, (8, D))

    v = jnp.where(row == 0, total(32), 0.0)
    v = jnp.where(row == 1, 0.5 * total(0), v)
    v = jnp.where(row == 2, total(8), v)
    v = jnp.where(row == 3, total(16), v)
    v = jnp.where(row == 4, total(24), v)
    vs[0] = v
    v_z = go(vs.at[0], vs.at[5], "z")

    turned(perm, dmt, dm)

    def tail_gemm(i, k, store):
        store(pl.ds(0, 256), nn(dmt[k][...], yv[:, 256 * i : 256 * i + 256]))
        store(pl.ds(256, 768), nn(xnt[k][...], dp[:, 768 * i : 768 * i + 768]))

    for i in range(2):
        ffn[i].made["c"].wait_send()

        def store(cols, t, i=i):
            here = pl.ds(i * WF + cols.start, cols.size)
            slots[0][:, :, :, here] = t.astype(BF16).reshape(4, 4, 32, cols.size)

        tail_gemm(i, 1, store)
        tail[i].core(slots[0].at[:, :, :, pl.ds(i * WF, WT)])

    def tail_keep(i):
        tail[i].arrived("c")
        tail_gemm(i, 0, lambda cols, t: into(s_t.at[i], cols, t))
        tail[i].e1()

    for i in range(4, 6):
        ffn[i].e2()
    for i in range(2):
        ffn[i].f1()
    tail_keep(0)
    tail_keep(1)
    v_z.wait_recv()
    vs[1] = vs[0] + jnp.where(row < 2, vs[5], 0.0)
    v_c = go(vs.at[1], vs.at[6], "c")
    for i in range(2, 4):
        ffn[i].f1()
    for i in range(2):
        tail[i].e2()
    for i in range(2):
        ffn[i].f2()
    v_c.wait_recv()
    vs[2] = vs[1] + vs[6]
    y, zh, x, c = place
    vx[x] = vs[2]
    v_x = [go(vs.at[2], vx.at[x], n) for n in ("xp", "xm", "x2")]
    for i in range(4, 6):
        ffn[i].f1()
    for i in range(2, 4):
        ffn[i].f2()

    z_dxn.wait_recv()
    z_rd.wait_recv()

    def tstep(t):
        rows = pl.ds(mult(t, 64), 64)
        r1 = r1v[rows, 0:1]
        d = own[rows, :] + xr[rows, :].astype(F32)
        q = rdr[rows, :].astype(F32)
        mean = (rd[rows, 0:1] + q[:, 0:1] + q[:, 64:65]) * (1.0 / D)
        xo = xv[rows, mine].astype(F32)
        tg[rows, :] += r1 * (d * g1[:, mine]) - xo * (r1 * r1 * r1 * mean)

    tiles(8, tstep)

    for i in range(4, 6):
        ffn[i].f2()
    for i in range(2):
        tail[i].f1()
    for w in v_x:
        w.wait_recv()
    vs[3] = (vx[0] + vx[1]) + (vx[2] + vx[3])
    vy[y] = vs[3]
    v_y = [go(vs.at[3], vy.at[y], n) for n in ("yp", "ym", "y2")]
    for i in range(6):
        ffn[i].hop()
    for i in range(2):
        tail[i].f2()
    for w in v_y:
        w.wait_recv()
    vs[4] = (vy[0] + vy[1]) + (vy[2] + vy[3])
    v_h = go(vs.at[4], vs.at[7], "zh")
    for i, o in enumerate((gate_o, up_o, down_o)):
        o[:, 0:WF] = ffn[2 * i].result()
        o[:, WF : 2 * WF] = ffn[2 * i + 1].result()
    for i in range(2):
        tail[i].hop()
    for i in range(2):
        t = tail[i].result()
        out_o[:, 256 * i : 256 * i + 256] = t[:, 0:256]
        in_o[:, 768 * i : 768 * i + 768] = t[:, 256:1024]
    v_h.wait_recv()
    vec_o[...] = vs[4] + vs[7]
    for q in made:
        if all(q is not d for d in (*z_m, z_out)):
            q.wait_send()
    for q in ffn + tail:
        q.finish()
    for q in ffn[2:] + tail:
        q.made["c"].wait_send()


def block(*args):
    hbm = pl.BlockSpec(memory_space=pl.ANY)
    vm = pl.BlockSpec(memory_space=pltpu.VMEM)
    sds = jax.ShapeDtypeStruct
    scratch = [
        pltpu.VMEM((2, 2, 4, 4, 32, FFH), BF16),
        pltpu.VMEM((FFH, D), BF16),
        pltpu.VMEM((D, 3 * HALF), BF16),
        pltpu.VMEM((HALF, D), BF16),
        pltpu.VMEM((ROWS, D), BF16),
        pltpu.VMEM((ROWS, D), BF16),
        pltpu.VMEM((ROWS, D), F32),
        pltpu.VMEM((ROWS, 3 * HALF), BF16),
        pltpu.VMEM((ROWS + 8, HALF), F32),
        pltpu.VMEM((ROWS, HALF), BF16),
        pltpu.VMEM((ROWS, FFH), BF16),
        pltpu.VMEM((ROWS, FFH), BF16),
        pltpu.VMEM((ROWS, FFH), BF16),
        pltpu.VMEM((ROWS, D), BF16),
        pltpu.VMEM((ROWS, D), BF16),
        pltpu.VMEM((ROWS, D), BF16),
        pltpu.VMEM((ROWS, D), BF16),
        pltpu.VMEM((ROWS + 8, HALF), F32),
        pltpu.VMEM((ROWS, 3 * HALF), BF16),
        pltpu.VMEM((ROWS, HALF), F32),
        pltpu.VMEM((ROWS, HALF), BF16),
        pltpu.VMEM((ROWS, HALF), BF16),
        pltpu.VMEM((ROWS, HALF), BF16),
        pltpu.VMEM((ROWS, 128), F32),
        pltpu.VMEM((ROWS, 128), BF16),
        pltpu.VMEM((ROWS, 128), BF16),
        pltpu.VMEM((ROWS, 128), F32),
        pltpu.VMEM((40, D), F32),
        pltpu.VMEM((8, 8, D), F32),
        pltpu.VMEM((4, 8, D), F32),
        pltpu.VMEM((4, 8, D), F32),
        pltpu.VMEM((8, HALF), F32),
        pltpu.VMEM((8, HALF), F32),
        *half_bufs(6, WF),
        *half_bufs(2, WT),
        pltpu.SemaphoreType.DMA((8,)),
        pltpu.SemaphoreType.DMA((8, len(KEYS))),
        pltpu.SemaphoreType.DMA((8, len(KEYS))),
        pltpu.SemaphoreType.DMA((24,)),
        pltpu.SemaphoreType.DMA((24,)),
    ]
    return pl.pallas_call(
        block_kernel,
        out_shape=(
            sds((ROWS, HALF), BF16),
            sds((ROWS, HALF), F32),
            sds((16, FFH), F32),
            sds((16, FFH), F32),
            sds((16, FFH), F32),
            sds((16, HALF), F32),
            sds((16, 3 * HALF), F32),
            sds((8, D), F32),
        ),
        in_specs=[hbm] * 7 + [vm] * 3,
        out_specs=(vm,) * 8,
        scratch_shapes=scratch,
        compiler_params=pltpu.CompilerParams(
            collective_id=1, has_side_effects=True, vmem_limit_bytes=VMEM_LIMIT
        ),
        cost_estimate=pl.CostEstimate(
            flops=32_000_000_000, bytes_accessed=24_000_000, transcendentals=0
        ),
        name="block",
    )(*args)


def body(
    tokens, norm_gain, in_weight, conv_weight, out_weight, ffn_gain, gate_weight, up_weight,
    down_weight, cotangent,
):
    bo, tg, gate_g, up_g, down_g, out_g, in_g, vec = block(
        tokens,
        cotangent,
        in_weight.reshape(D, -1),
        out_weight,
        gate_weight.reshape(2, 4, 4, 32, FFH),
        up_weight.reshape(2, 4, 4, 32, FFH),
        down_weight,
        conv_weight.astype(F32),
        norm_gain.astype(F32)[None],
        ffn_gain.astype(F32)[None],
    )
    return (
        bo,
        tg,
        vec[0],
        in_g.reshape(16, 3, HALF),
        vec[2:5, :HALF],
        out_g.T,
        vec[1],
        gate_g,
        up_g,
        down_g.T,
    )


def solution(mesh):
    return jax.shard_map(
        body,
        mesh=mesh,
        in_specs=(
            P("seq", "shard"),
            P(),
            P(None, None, "shard"),
            P(None, "shard"),
            P("shard", None),
            P(),
            P(None, "shard"),
            P(None, "shard"),
            P("shard", None),
            P("seq", "shard"),
        ),
        out_specs=(
            P("seq", "shard"),
            P("seq", "shard"),
            P(),
            P("seq", None, "shard"),
            P(None, "shard"),
            P("shard", "seq"),
            P(),
            P("seq", "shard"),
            P("seq", "shard"),
            P("shard", "seq"),
        ),
        check_vma=False,
    )
```

```python
import jax
import jax.numpy as jnp
from jax import lax
from jax.experimental import pallas as pl
from jax.experimental.pallas import tpu as pltpu
from jax.sharding import PartitionSpec as P

SEQS = 2
NORM_EPS = 1e-05
MESH = pl.DeviceIdType.MESH
F32 = jnp.float32
BF16 = jnp.bfloat16
VMEM_LIMIT = 67_000_000

ROWS = 512
D = 1024
HALF = 512
FFH = 2304
WF = 1152
WT = 1024
KEYS = ("c", "e1p", "e1m", "e2p", "e2m", "f1p", "f1m", "f2p", "f2m", "h")


def nt(a, b):
    return lax.dot_general(a, b, (((1,), (1,)), ((), ())), preferred_element_type=F32)


def nn(a, b):
    return jnp.dot(a, b, preferred_element_type=F32)


def mod(a, n):
    return lax.rem(a, n)


def neighbours():
    s = lax.axis_index("seq")
    sh = lax.axis_index("shard")
    y, zh, x, c = s // 16, mod(s // 8, 2), mod(s // 2, 4), mod(s, 2)

    def at(y_, zh_, x_, c_):
        return (((y_ * 2 + zh_) * 4 + x_) * 2 + c_, sh)

    to = {
        "z": (s, 1 - sh),
        "c": at(y, zh, x, 1 - c),
        "xp": at(y, zh, mod(x + 1, 4), c),
        "xm": at(y, zh, mod(x + 3, 4), c),
        "x2": at(y, zh, mod(x + 2, 4), c),
        "yp": at(mod(y + 1, 4), zh, x, c),
        "ym": at(mod(y + 3, 4), zh, x, c),
        "y2": at(mod(y + 2, 4), zh, x, c),
        "zh": at(y, 1 - zh, x, c),
        "nx": (mod(s + 1, 64), sh),
        "pv": (mod(s + 63, 64), sh),
    }
    return s, sh, (y, zh, x, c), to


def greet(to, names):
    barrier = pltpu.get_barrier_semaphore()
    for name in names:
        pl.semaphore_signal(barrier, inc=1, device_id=to[name], device_id_type=MESH)
    pl.semaphore_wait(barrier, len(names))


def send(src, dst, sems, rems, device):
    return pltpu.make_async_remote_copy(
        src_ref=src,
        dst_ref=dst,
        send_sem=sems,
        recv_sem=rems,
        device_id=device,
        device_id_type=MESH,
    )


def added(dst, *others):
    blocks = dst.shape[0]

    def step(i, _):
        total = dst[i].astype(F32)
        for o in others:
            total = total + o[i].astype(F32)
        dst[i] = total.astype(BF16)
        return 0

    lax.fori_loop(0, blocks, step, 0)


class Half:
    def __init__(self, first, to, s_ref, bufs, sems, rems):
        self.first, self.to, self.s, self.b = first, to, s_ref, bufs
        self.sems, self.rems = sems, rems
        self.ups = ("xp", "xm", "yp", "ym") if first == 0 else ("yp", "ym", "xp", "xm")
        self.sent = []
        self.made = {}

    def view(self, i, j):
        i, j = (i, j) if self.first == 0 else (j, i)
        i = slice(None) if i is None else (pl.ds(*i) if isinstance(i, tuple) else i)
        j = slice(None) if j is None else (pl.ds(*j) if isinstance(j, tuple) else j)
        return self.s.at[i, j]

    def go(self, key, src, dst, name):
        k = KEYS.index(key)
        copy = send(src, dst, self.sems.at[k], self.rems.at[k], self.to[name])
        copy.start()
        self.made[key] = copy

    def arrived(self, *keys):
        for k in keys:
            self.made[k].wait_recv()

    def core(self, g_ref):
        self.go("c", g_ref, self.s, "c")

    def e1(self):
        self.go("e1p", self.view(2, (0, 2)), self.b["e1p"], self.ups[0])
        self.go("e1m", self.view(2, (2, 2)), self.b["e1m"], self.ups[1])

    def e2(self):
        self.arrived("e1p", "e1m")
        added(self.view(1, (0, 2)), self.b["e1p"])
        self.go("e2p", self.view(1, None), self.b["e2p"], self.ups[0])
        added(self.view(3, (2, 2)), self.b["e1m"])
        self.go("e2m", self.view(3, None), self.b["e2m"], self.ups[1])

    def f1(self):
        self.arrived("e2p", "e2m")
        added(self.view(0, None), self.b["e2p"], self.b["e2m"])
        t = self.view(0, 2)
        self.go("f1p", t.at[pl.ds(0, 16)], self.b["f1p"], self.ups[2])
        self.go("f1m", t.at[pl.ds(16, 16)], self.b["f1m"], self.ups[3])

    def f2(self):
        self.arrived("f1p", "f1m")
        t1, t3 = self.view(0, 1), self.view(0, 3)
        t1[0:16, :] = (t1[0:16, :].astype(F32) + self.b["f1p"][...].astype(F32)).astype(BF16)
        self.go("f2p", t1, self.b["f2p"], self.ups[2])
        t3[16:32, :] = (t3[16:32, :].astype(F32) + self.b["f1m"][...].astype(F32)).astype(BF16)
        self.go("f2m", t3, self.b["f2m"], self.ups[3])

    def hop(self):
        self.arrived("f2p", "f2m")
        t = self.view(0, 0)
        t[...] = (
            t[...].astype(F32) + self.b["f2p"][...].astype(F32) + self.b["f2m"][...].astype(F32)
        ).astype(BF16)
        self.go("h", t.at[pl.ds(16, 16)], self.b["h"], "zh")

    def result(self):
        self.arrived("h")
        return self.view(0, 0)[0:16, :].astype(F32) + self.b["h"][...].astype(F32)

    def finish(self):
        for k in KEYS:
            if k != "c":
                self.made[k].wait_send()


def half_bufs(n, w):
    return [
        pltpu.VMEM((n, 4, 4, 32, w), BF16),
        pltpu.VMEM((n, 2, 2, 32, w), BF16),
        pltpu.VMEM((n, 2, 4, 32, w), BF16),
        pltpu.VMEM((n, 2, 16, w), BF16),
        pltpu.VMEM((n, 2, 32, w), BF16),
        pltpu.VMEM((n, 16, w), BF16),
    ]


def halves(n, to, refs, sems, rems, base):
    s, e1, e2, f1, f2, h = refs
    out = []
    for i in range(n):
        bufs = {
            "e1p": e1.at[i, 0],
            "e1m": e1.at[i, 1],
            "e2p": e2.at[i, 0],
            "e2m": e2.at[i, 1],
            "f1p": f1.at[i, 0],
            "f1m": f1.at[i, 1],
            "f2p": f2.at[i, 0],
            "f2m": f2.at[i, 1],
            "h": h.at[i],
        }
        out.append(Half(i % 2, to, s.at[i], bufs, sems.at[base + i], rems.at[base + i]))
    return out


def tiles(n, body):
    lax.fori_loop(0, n, lambda i, _: (body(i), 0)[1], 0)


def mult(i, n):
    return pl.multiple_of(i * n, n)


def flat(v):
    return v.reshape(-1, v.shape[-1])


def turned(perm, at, a_ref):
    for k in range(2):
        at[k][...] = nt(perm[k], a_ref[...]).astype(BF16)


def order_matrix(perm, place):
    y, zh, x, c = place
    k = lax.broadcasted_iota(jnp.int32, (1, D), 1)
    k16 = k >> 4
    crel = ((k16 & 1) - c) & 1
    xrel = (((k16 >> 1) & 3) - x) & 3
    zrel = (((k16 >> 3) & 1) - zh) & 1
    yrel = ((k16 >> 4) - y) & 3
    pos = (((crel * 4 + xrel) * 4 + yrel) * 2 + zrel) * 16 + (k & 15)

    for b in range(2):

        def step(t, b=b):
            r = lax.broadcasted_iota(jnp.int32, (64, D), 0) + (b * 512 + t * 64)
            perm[b, pl.ds(mult(t, 64), 64), :] = jnp.where(r == pos, 1.0, 0.0).astype(BF16)

        tiles(8, step)


def block_kernel(
    tok_in, cot_in, win_in, wout_in, wg_in, wu_in, wd_in, cw_in, g1_in, g2_in,
    bo, tg, gate_o, up_o, down_o, out_o, in_o, ng_o, fg_o, cg_o,
    wbuf, wd, win, wout, xv, cot, hv, p, bx, yv, u, da, db, dm, dsend, drecv, mrecv,
    dce, perm, xnt, own, xs, xr, br, rd, rds, rdr, r1v, acc, vs, vx, vy, halo_p, halo_n,
    s_f, e1_f, e2_f, f1_f, f2_f, h_f, s_t, e1_t, e2_t, f1_t, f2_t, h_t,
    cw, g1, g2, lsem, rs_s, rs_r, ms, mr,
):
    s, sh, place, to = neighbours()
    mine = pl.ds(mult(sh, 512), 512)
    theirs = pl.ds(mult(1 - sh, 512), 512)
    loads = []

    def load(src, dst):
        copy = pltpu.make_async_copy(src, dst, lsem.at[len(loads)])
        copy.start()
        loads.append(copy)
        return copy

    made = []

    def go(src, dst, name):
        k = len(made)
        copy = send(src, dst, ms.at[k], mr.at[k], to[name])
        copy.start()
        made.append(copy)
        return copy

    l_tok = load(tok_in, xv.at[:, mine])
    l_win = [load(win_in.at[j], win.at[:, pl.ds(512 * j, 512)]) for j in range(3)]
    greet(to, ("z", "c", "xp", "xm", "x2", "yp", "ym", "y2", "zh", "nx", "pv"))
    parts = [pl.ds(0, 256), pl.ds(256, 256)]
    z_tok = [None, None]
    for r in (1, 0):
        z_tok[r] = go(tok_in.at[parts[r]], xv.at[parts[r], mine], "z")

    cw[0:3, :] = cw_in[...].astype(F32)
    g1[...] = g1_in[...].astype(F32).reshape(1, D)
    g2[...] = g2_in[...].astype(F32).reshape(1, D)
    l_wout = load(wout_in, wout)
    l_tok.wait()
    for l in l_win:
        l.wait()

    def project(r):

        def step(t):
            rows = pl.ds(pl.multiple_of(r * 256 + t * 32, 32), 32)
            xf = xv[rows, :].astype(F32)
            r1 = lax.rsqrt(jnp.mean(xf * xf, axis=-1, keepdims=True) + NORM_EPS)
            r1v[rows, :] = jnp.broadcast_to(r1, (32, 128))
            dm[rows, :] = (xf * r1 * g1[...]).astype(BF16)

        tiles(8, step)
        rows = parts[r]
        for n in range(2):
            c = 256 * n
            tb = nn(dm[rows, :], win[:, c : c + 256])
            tx = nn(dm[rows, :], win[:, 1024 + c : 1280 + c])
            p[rows, c : c + 256] = tb.astype(BF16)
            p[rows, 1024 + c : 1280 + c] = tx.astype(BF16)
            bx[pl.ds(8 + 256 * r, 256), c : c + 256] = tb * tx
            tc = nn(dm[rows, :], win[:, 512 + c : 768 + c])
            own[rows, c : c + 256] = tc
            p[rows, 512 + c : 768 + c] = tc.astype(BF16)

    z_tok[1].wait_recv()
    l_cot = load(cot_in, cot.at[:, mine])
    l_wg = load(wg_in, wbuf.at[0])
    l_wu = load(wu_in, wbuf.at[1])
    l_wd = load(wd_in, wd)
    project(1)
    z_halo = go(bx.at[pl.ds(512, 8)], halo_p, "nx")
    z_tok[0].wait_recv()
    z_cot = go(cot_in, cot.at[:, mine], "z")
    project(0)
    z_halo.wait_recv()
    bx[0:8, :] = jnp.where(mod(s, 32) == 0, 0.0, halo_p[...])
    l_wout.wait()
    z_m = []
    for r in range(2):

        def step(t, r=r):
            base = r * 256 + t * 64
            w = bx[pl.ds(pl.multiple_of(base, 64), 72), :]
            conv = cw[0:1, :] * w[6:70] + cw[1:2, :] * w[7:71] + cw[2:3, :] * w[8:72]
            rows = pl.ds(pl.multiple_of(base, 64), 64)
            yv[rows, :] = (own[rows, :] * conv).astype(BF16)

        tiles(4, step)
        rows = parts[r]
        for n in range(2):
            cols = pl.ds(512 * n, 512)
            dsend[rows, cols] = nn(yv[rows, :], wout[:, cols]).astype(BF16)
        z_m.append(go(dsend.at[rows], mrecv.at[rows], "z"))

    order_matrix(perm, place)
    turned(perm, [xnt.at[0], xnt.at[1]], dm)

    l_cot.wait()
    z_cot.wait_recv()
    for l in (l_wg, l_wu, l_wd):
        l.wait()
    z_dhn = []
    for r in range(2):
        z_m[r].wait_recv()

        def step(t, r=r):
            rows = pl.ds(pl.multiple_of(r * 256 + t * 32, 32), 32)
            hf = xv[rows, :].astype(F32) + dsend[rows, :].astype(F32) + mrecv[rows, :].astype(F32)
            hv[rows, :] = hf.astype(BF16)
            r2 = lax.rsqrt(jnp.mean(hf * hf, axis=-1, keepdims=True) + NORM_EPS)
            dm[rows, :] = (hf * r2 * g2[...]).astype(BF16)

        tiles(8, step)
        rows = parts[r]
        for n in range(9):
            cols = pl.ds(256 * n, 256)
            a = nn(dm[rows, :], flat(wbuf[0, :, :, :, :, cols]))
            b = nn(dm[rows, :], flat(wbuf[1, :, :, :, :, cols]))
            du = nt(cot[rows, :], wd[cols, :])
            sig = jax.nn.sigmoid(a)
            silu = a * sig
            u[rows, cols] = (silu * b).astype(BF16)
            db[rows, cols] = (du * silu).astype(BF16)
            da[rows, cols] = (du * b * (sig + silu * (1.0 - sig))).astype(BF16)
        z_m[r].wait_send()
        for n in range(2):
            t = nt(da[rows, :], flat(wbuf[0, n])) + nt(db[rows, :], flat(wbuf[1, n]))
            dsend[rows, pl.ds(512 * n, 512)] = t.astype(BF16)
        z_dhn.append(go(dsend.at[rows], drecv.at[rows], "z"))

    hnt = [mrecv.at[:, pl.ds(512 * k, 512)] for k in range(2)]
    cott = [wd.at[pl.ds(0, 512), pl.ds(512 * k, 512)] for k in range(2)]
    dmt = [wd.at[pl.ds(512, 512), pl.ds(512 * k, 512)] for k in range(2)]
    dp = wbuf.at[1, 1]
    turned(perm, hnt, dm)
    ffn = halves(6, to, (s_f, e1_f, e2_f, f1_f, f2_f, h_f), rs_s, rs_r, 0)
    tail = halves(2, to, (s_t, e1_t, e2_t, f1_t, f2_t, h_t), rs_s, rs_r, 6)
    ffn_parts = [(hnt, da), (hnt, db), (cott, u)]
    slots = [wbuf.at[0, 0], wbuf.at[0, 1], wbuf.at[1, 0]]

    def ffn_send(k):
        at, b = ffn_parts[k]
        for n in range(3):
            cols = pl.ds(768 * n, 768)
            t = nn(at[1][...], b[:, cols])
            slots[k][:, :, :, cols] = t.astype(BF16).reshape(4, 4, 32, 768)
            if n == 1:
                ffn[2 * k].core(slots[k].at[:, :, :, pl.ds(0, WF)])
        ffn[2 * k + 1].core(slots[k].at[:, :, :, pl.ds(WF, WF)])

    def into(ref, cols, t):
        ref[:, :, :, cols] = (
            t.reshape(4, 4, 32, t.shape[-1]) + ref[:, :, :, cols].astype(F32)
        ).astype(BF16)

    def ffn_keep(k):
        at, b = ffn_parts[k]
        lo, hi = s_f.at[2 * k], s_f.at[2 * k + 1]
        ffn[2 * k].arrived("c")
        t = nn(at[0][...], b[:, 0:768])
        into(lo, pl.ds(0, 768), t)
        ffn[2 * k + 1].arrived("c")
        t = nn(at[0][...], b[:, 768:1536])
        into(lo, pl.ds(768, 384), t[:, 0:384])
        ffn[2 * k].e1()
        into(hi, pl.ds(0, 384), t[:, 384:768])
        t = nn(at[0][...], b[:, 1536:2304])
        into(hi, pl.ds(384, 768), t)
        ffn[2 * k + 1].e1()

    ffn_send(0)
    ffn_send(1)
    xs[...] = nn(u[...], wd[:, theirs]).astype(BF16)
    bo[...] = (nn(u[...], wd[:, mine]) + hv[:, mine].astype(F32)).astype(BF16)
    ffn_keep(0)

    acc[...] = jnp.zeros_like(acc)

    def mixer(r):

        def step(t):
            rows = pl.ds(pl.multiple_of(r * 256 + t * 32, 32), 32)
            hf = hv[rows, :].astype(F32)
            r2 = lax.rsqrt(jnp.mean(hf * hf, axis=-1, keepdims=True) + NORM_EPS)
            dhn = dsend[rows, :].astype(F32) + drecv[rows, :].astype(F32)
            acc[0:8, :] += (dhn * hf * r2).reshape(4, 8, D).sum(axis=0)
            scaled = dhn * g2[...]
            dot = jnp.mean(scaled * hf, axis=-1, keepdims=True)
            d = cot[rows, :].astype(F32) + r2 * scaled - hf * (r2 * r2 * r2 * dot)
            dm[rows, :] = d.astype(BF16)
            tg[rows, :] = jnp.where(sh == 0, d[:, 0:512], d[:, 512:1024])

        tiles(8, step)
        rows = parts[r]
        dy = nt(dm[rows, :], wout[...])
        own[rows, :] = dy
        dce[rows, :] = dy * p[rows, 512:1024].astype(F32)

    z_dhn[0].wait_recv()
    mixer(0)
    back = go(dce.at[pl.ds(0, 8)], halo_n, "pv")
    ffn_keep(1)
    turned(perm, cott, cot)
    ffn_send(2)
    for i in range(2):
        ffn[i].e2()
    z_dhn[1].wait_recv()
    z_out = go(xs, br, "z")
    mixer(1)
    back.wait_recv()
    dce[512:520, :] = jnp.where(mod(s, 32) == 31, 0.0, halo_n[...])

    def dstep(t):
        rows = pl.ds(mult(t, 64), 64)
        ext = pl.ds(mult(t, 64), 72)
        dc = dce[ext, :]
        w = bx[ext, :]
        d0 = dc[0:64]
        b2, b1, b0 = w[6:70], w[7:71], w[8:72]
        acc[8:16, 0:512] += (d0 * b2).reshape(8, 8, 512).sum(axis=0)
        acc[16:24, 0:512] += (d0 * b1).reshape(8, 8, 512).sum(axis=0)
        acc[24:32, 0:512] += (d0 * b0).reshape(8, 8, 512).sum(axis=0)
        conv = cw[0:1, :] * b2 + cw[1:2, :] * b1 + cw[2:3, :] * b0
        dbx = cw[2:3, :] * d0 + cw[1:2, :] * dc[1:65] + cw[0:1, :] * dc[2:66]
        at = (t // 2, pl.ds(mod(t, 2) * 2, 2))

        def put(col, v):
            dp[at[0], at[1], :, col : col + 512] = v.astype(BF16).reshape(2, 32, 512)

        put(0, dbx * p[rows, 1024:1536].astype(F32))
        put(512, own[rows, :] * conv)
        put(1024, dbx * p[rows, 0:512].astype(F32))

    tiles(8, dstep)

    rd[...] = jnp.zeros_like(rd)

    def dxn(half, dst):
        for n in range(2):
            wr = pl.ds(pl.multiple_of(half * 512 + n * 256, 256), 256)
            for r, rows in enumerate(parts):
                t = nt(flat(dp[2 * r : 2 * r + 2, :, :, 0:1536]), win[wr, :])
                tx = t * xv[rows, wr].astype(F32)
                rd[rows, :] += jnp.broadcast_to(
                    jnp.sum(tx * g1[:, wr], axis=-1, keepdims=True), (256, 128)
                )
                acc[32:40, wr] += (tx * r1v[rows, 0:1]).reshape(32, 8, 256).sum(axis=0)
                dst[rows, pl.ds(256 * n, 256)] = t.astype(dst.dtype)

    dxn(1 - sh, mrecv.at[:, pl.ds(0, 512)])
    z_dxn = go(mrecv.at[:, pl.ds(0, 512)], xr, "z")
    for i in range(2, 4):
        ffn[i].e2()
    dxn(sh, own)
    hi = rd[...].astype(BF16)
    lo = (rd[...] - hi.astype(F32)).astype(BF16)
    lane = lax.broadcasted_iota(jnp.int32, (ROWS, 128), 1)
    rds[...] = jnp.where(lane < 64, hi.astype(F32), lo.astype(F32)).astype(BF16)
    z_rd = go(rds, rdr, "z")

    row = lax.broadcasted_iota(jnp.int32, (8, D), 0)

    def total(lo_):
        t = jnp.sum(acc[lo_ : lo_ + 8, :], axis=0, keepdims=True)
        return jnp.broadcast_to(t, (8, D))

    v = jnp.where(row == 0, total(32), 0.0)
    v = jnp.where(row == 1, 0.5 * total(0), v)
    v = jnp.where(row == 2, total(8), v)
    v = jnp.where(row == 3, total(16), v)
    v = jnp.where(row == 4, total(24), v)
    vs[0] = v
    v_z = go(vs.at[0], vs.at[5], "z")

    turned(perm, dmt, dm)

    def tail_gemm(i, k, store):
        store(pl.ds(0, 256), nn(dmt[k][...], yv[:, 256 * i : 256 * i + 256]))
        store(pl.ds(256, 768), nn(xnt[k], flat(dp[:, :, :, 768 * i : 768 * i + 768])))

    for i in range(2):
        ffn[i].made["c"].wait_send()

        def store(cols, t, i=i):
            here = pl.ds(i * WF + cols.start, cols.size)
            slots[0][:, :, :, here] = t.astype(BF16).reshape(4, 4, 32, cols.size)

        tail_gemm(i, 1, store)
        tail[i].core(slots[0].at[:, :, :, pl.ds(i * WF, WT)])

    def tail_keep(i):
        tail[i].arrived("c")
        tail_gemm(i, 0, lambda cols, t: into(s_t.at[i], cols, t))
        tail[i].e1()

    ffn_keep(2)
    for i in range(2):
        ffn[i].f1()
    tail_keep(0)
    tail_keep(1)
    for i in range(4, 6):
        ffn[i].e2()
    v_z.wait_recv()
    vs[1] = vs[0] + jnp.where(row < 2, vs[5], 0.0)
    v_c = go(vs.at[1], vs.at[6], "c")
    for i in range(2, 4):
        ffn[i].f1()
    for i in range(2):
        tail[i].e2()
    for i in range(2):
        ffn[i].f2()
    v_c.wait_recv()
    vs[2] = vs[1] + vs[6]
    y, zh, x, c = place
    vx[x] = vs[2]
    v_x = [go(vs.at[2], vx.at[x], n) for n in ("xp", "xm", "x2")]
    for i in range(4, 6):
        ffn[i].f1()
    for i in range(2, 4):
        ffn[i].f2()

    z_dxn.wait_recv()
    z_rd.wait_recv()

    def tstep(t):
        rows = pl.ds(mult(t, 64), 64)
        r1 = r1v[rows, 0:1]
        d = own[rows, :] + xr[rows, :].astype(F32)
        q = rdr[rows, :].astype(F32)
        mean = (rd[rows, 0:1] + q[:, 0:1] + q[:, 64:65]) * (1.0 / D)
        xo = xv[rows, mine].astype(F32)
        tg[rows, :] += r1 * (d * g1[:, mine]) - xo * (r1 * r1 * r1 * mean)

    tiles(8, tstep)
    z_out.wait_recv()
    bo[...] = (bo[...].astype(F32) + br[...].astype(F32)).astype(BF16)

    for i in range(4, 6):
        ffn[i].f2()
    for i in range(2):
        tail[i].f1()
    for w in v_x:
        w.wait_recv()
    vs[3] = (vx[0] + vx[1]) + (vx[2] + vx[3])
    vy[y] = vs[3]
    v_y = [go(vs.at[3], vy.at[y], n) for n in ("yp", "ym", "y2")]
    for i in range(6):
        ffn[i].hop()
    for i in range(2):
        tail[i].f2()
    for w in v_y:
        w.wait_recv()
    vs[4] = (vy[0] + vy[1]) + (vy[2] + vy[3])
    v_h = go(vs.at[4], vs.at[7], "zh")
    for i, o in enumerate((gate_o, up_o, down_o)):
        o[:, 0:WF] = ffn[2 * i].result()
        o[:, WF : 2 * WF] = ffn[2 * i + 1].result()
    for i in range(2):
        tail[i].hop()
    for i in range(2):
        t = tail[i].result()
        out_o[:, 256 * i : 256 * i + 256] = t[:, 0:256]
        for j in range(6):
            n = 768 * i + 128 * j
            in_o[n // 512, :, n % 512 : n % 512 + 128] = t[:, 256 + 128 * j : 384 + 128 * j]
    v_h.wait_recv()
    v = vs[4] + vs[7]
    ng_o[...] = v[0:1, :]
    fg_o[...] = v[1:2, :]
    cg_o[...] = v[2:5, 0:512]
    for q in made:
        if all(q is not d for d in z_m):
            q.wait_send()
    for q in ffn + tail:
        q.finish()
    for q in ffn[2:] + tail:
        q.made["c"].wait_send()


def block(*args):
    hbm = pl.BlockSpec(memory_space=pl.ANY)
    vm = pl.BlockSpec(memory_space=pltpu.VMEM)
    sds = jax.ShapeDtypeStruct
    scratch = [
        pltpu.VMEM((2, 2, 4, 4, 32, FFH), BF16),
        pltpu.VMEM((FFH, D), BF16),
        pltpu.VMEM((D, 3 * HALF), BF16),
        pltpu.VMEM((HALF, D), BF16),
        pltpu.VMEM((ROWS, D), BF16),
        pltpu.VMEM((ROWS, D), BF16),
        pltpu.VMEM((ROWS, D), BF16),
        pltpu.VMEM((ROWS, 3 * HALF), BF16),
        pltpu.VMEM((ROWS + 8, HALF), F32),
        pltpu.VMEM((ROWS, HALF), BF16),
        pltpu.VMEM((ROWS, FFH), BF16),
        pltpu.VMEM((ROWS, FFH), BF16),
        pltpu.VMEM((ROWS, FFH), BF16),
        pltpu.VMEM((ROWS, D), BF16),
        pltpu.VMEM((ROWS, D), BF16),
        pltpu.VMEM((ROWS, D), BF16),
        pltpu.VMEM((ROWS, D), BF16),
        pltpu.VMEM((ROWS + 8, HALF), F32),
        pltpu.VMEM((2, HALF, D), BF16),
        pltpu.VMEM((2, HALF, ROWS), BF16),
        pltpu.VMEM((ROWS, HALF), F32),
        pltpu.VMEM((ROWS, HALF), BF16),
        pltpu.VMEM((ROWS, HALF), BF16),
        pltpu.VMEM((ROWS, HALF), BF16),
        pltpu.VMEM((ROWS, 128), F32),
        pltpu.VMEM((ROWS, 128), BF16),
        pltpu.VMEM((ROWS, 128), BF16),
        pltpu.VMEM((ROWS, 128), F32),
        pltpu.VMEM((40, D), F32),
        pltpu.VMEM((8, 8, D), F32),
        pltpu.VMEM((4, 8, D), F32),
        pltpu.VMEM((4, 8, D), F32),
        pltpu.VMEM((8, HALF), F32),
        pltpu.VMEM((8, HALF), F32),
        *half_bufs(6, WF),
        *half_bufs(2, WT),
        pltpu.VMEM((8, HALF), F32),
        pltpu.VMEM((1, D), F32),
        pltpu.VMEM((1, D), F32),
        pltpu.SemaphoreType.DMA((16,)),
        pltpu.SemaphoreType.DMA((8, len(KEYS))),
        pltpu.SemaphoreType.DMA((8, len(KEYS))),
        pltpu.SemaphoreType.DMA((24,)),
        pltpu.SemaphoreType.DMA((24,)),
    ]
    return pl.pallas_call(
        block_kernel,
        out_shape=(
            sds((ROWS, HALF), BF16),
            sds((ROWS, HALF), F32),
            sds((16, FFH), F32),
            sds((16, FFH), F32),
            sds((16, FFH), F32),
            sds((16, HALF), F32),
            sds((3, 16, HALF), F32),
            sds((1, D), F32),
            sds((1, D), F32),
            sds((3, HALF), F32),
        ),
        in_specs=[hbm] * 7 + [vm] * 3,
        out_specs=(vm,) * 10,
        scratch_shapes=scratch,
        compiler_params=pltpu.CompilerParams(
            collective_id=1, has_side_effects=True, vmem_limit_bytes=VMEM_LIMIT
        ),
        cost_estimate=pl.CostEstimate(
            flops=32_000_000_000, bytes_accessed=24_000_000, transcendentals=0
        ),
        name="block",
    )(*args)


def settle_kernel(*refs):
    n = len(refs) // 2
    for i in range(n):
        refs[n + i][...] = refs[i][...]


def settle(arrays):
    n = len(arrays)
    vm = pl.BlockSpec(memory_space=pltpu.VMEM)
    return pl.pallas_call(
        settle_kernel,
        out_shape=tuple(jax.ShapeDtypeStruct(a.shape, a.dtype) for a in arrays),
        in_specs=[vm] * n,
        out_specs=(vm,) * n,
        compiler_params=pltpu.CompilerParams(vmem_limit_bytes=VMEM_LIMIT),
        name="settle",
    )(*arrays)


def body(
    tokens, norm_gain, in_weight, conv_weight, out_weight, ffn_gain, gate_weight, up_weight,
    down_weight, cotangent,
):
    bo, tg, gate_g, up_g, down_g, out_g, in_g, ng, fg, cg = settle(
        block(
            tokens,
            cotangent,
            in_weight.transpose(1, 0, 2),
            out_weight,
            gate_weight.reshape(2, 4, 4, 32, FFH),
            up_weight.reshape(2, 4, 4, 32, FFH),
            down_weight,
            conv_weight,
            norm_gain,
            ffn_gain,
        )
    )
    return (
        bo,
        tg,
        ng.reshape(D),
        in_g.transpose(1, 0, 2),
        cg,
        out_g.T,
        fg.reshape(D),
        gate_g,
        up_g,
        down_g.T,
    )


def solution(mesh):
    return jax.shard_map(
        body,
        mesh=mesh,
        in_specs=(
            P("seq", "shard"),
            P(),
            P(None, None, "shard"),
            P(None, "shard"),
            P("shard", None),
            P(),
            P(None, "shard"),
            P(None, "shard"),
            P("shard", None),
            P("seq", "shard"),
        ),
        out_specs=(
            P("seq", "shard"),
            P("seq", "shard"),
            P(),
            P("seq", None, "shard"),
            P(None, "shard"),
            P("shard", "seq"),
            P(),
            P("seq", "shard"),
            P("seq", "shard"),
            P("shard", "seq"),
        ),
        check_vma=False,
    )
```

```python
import jax
import jax.numpy as jnp
from jax import lax
from jax.experimental import pallas as pl
from jax.experimental.pallas import tpu as pltpu
from jax.sharding import PartitionSpec as P

SEQS = 2
NORM_EPS = 1e-05
MESH = pl.DeviceIdType.MESH
F32 = jnp.float32
BF16 = jnp.bfloat16
VMEM_LIMIT = 67_000_000

ROWS = 512
D = 1024
HALF = 512
FFH = 2304
WF = 1152
WT = 1024
KEYS = ("c", "e1p", "e1m", "e2p", "e2m", "f1p", "f1m", "f2p", "f2m", "h")


def nt(a, b):
    return lax.dot_general(a, b, (((1,), (1,)), ((), ())), preferred_element_type=F32)


def nn(a, b):
    return jnp.dot(a, b, preferred_element_type=F32)


def mod(a, n):
    return lax.rem(a, n)


def neighbours():
    s = lax.axis_index("seq")
    sh = lax.axis_index("shard")
    y, zh, x, c = s // 16, mod(s // 8, 2), mod(s // 2, 4), mod(s, 2)

    def at(y_, zh_, x_, c_):
        return (((y_ * 2 + zh_) * 4 + x_) * 2 + c_, sh)

    to = {
        "z": (s, 1 - sh),
        "c": at(y, zh, x, 1 - c),
        "xp": at(y, zh, mod(x + 1, 4), c),
        "xm": at(y, zh, mod(x + 3, 4), c),
        "x2": at(y, zh, mod(x + 2, 4), c),
        "yp": at(mod(y + 1, 4), zh, x, c),
        "ym": at(mod(y + 3, 4), zh, x, c),
        "y2": at(mod(y + 2, 4), zh, x, c),
        "zh": at(y, 1 - zh, x, c),
        "nx": (mod(s + 1, 64), sh),
        "pv": (mod(s + 63, 64), sh),
    }
    return s, sh, (y, zh, x, c), to


def greet(to, names):
    barrier = pltpu.get_barrier_semaphore()
    for name in names:
        pl.semaphore_signal(barrier, inc=1, device_id=to[name], device_id_type=MESH)
    pl.semaphore_wait(barrier, len(names))


def send(src, dst, sems, rems, device):
    return pltpu.make_async_remote_copy(
        src_ref=src,
        dst_ref=dst,
        send_sem=sems,
        recv_sem=rems,
        device_id=device,
        device_id_type=MESH,
    )


def added(dst, *others):
    blocks = dst.shape[0]

    def step(i, _):
        total = dst[i].astype(F32)
        for o in others:
            total = total + o[i].astype(F32)
        dst[i] = total.astype(BF16)
        return 0

    lax.fori_loop(0, blocks, step, 0)


class Half:
    def __init__(self, first, to, s_ref, bufs, sems, rems):
        self.first, self.to, self.s, self.b = first, to, s_ref, bufs
        self.sems, self.rems = sems, rems
        self.ups = ("xp", "xm", "yp", "ym") if first == 0 else ("yp", "ym", "xp", "xm")
        self.sent = []
        self.made = {}

    def view(self, i, j):
        i, j = (i, j) if self.first == 0 else (j, i)
        i = slice(None) if i is None else (pl.ds(*i) if isinstance(i, tuple) else i)
        j = slice(None) if j is None else (pl.ds(*j) if isinstance(j, tuple) else j)
        return self.s.at[i, j]

    def go(self, key, src, dst, name):
        k = KEYS.index(key)
        copy = send(src, dst, self.sems.at[k], self.rems.at[k], self.to[name])
        copy.start()
        self.made[key] = copy

    def arrived(self, *keys):
        for k in keys:
            self.made[k].wait_recv()

    def core(self, g_ref):
        self.go("c", g_ref, self.s, "c")

    def e1(self):
        self.go("e1p", self.view(2, (0, 2)), self.b["e1p"], self.ups[0])
        self.go("e1m", self.view(2, (2, 2)), self.b["e1m"], self.ups[1])

    def e2(self):
        self.arrived("e1p", "e1m")
        added(self.view(1, (0, 2)), self.b["e1p"])
        self.go("e2p", self.view(1, None), self.b["e2p"], self.ups[0])
        added(self.view(3, (2, 2)), self.b["e1m"])
        self.go("e2m", self.view(3, None), self.b["e2m"], self.ups[1])

    def f1(self):
        self.arrived("e2p", "e2m")
        added(self.view(0, None), self.b["e2p"], self.b["e2m"])
        t = self.view(0, 2)
        self.go("f1p", t.at[pl.ds(0, 16)], self.b["f1p"], self.ups[2])
        self.go("f1m", t.at[pl.ds(16, 16)], self.b["f1m"], self.ups[3])

    def f2(self):
        self.arrived("f1p", "f1m")
        t1, t3 = self.view(0, 1), self.view(0, 3)
        t1[0:16, :] = (t1[0:16, :].astype(F32) + self.b["f1p"][...].astype(F32)).astype(BF16)
        self.go("f2p", t1, self.b["f2p"], self.ups[2])
        t3[16:32, :] = (t3[16:32, :].astype(F32) + self.b["f1m"][...].astype(F32)).astype(BF16)
        self.go("f2m", t3, self.b["f2m"], self.ups[3])

    def hop(self):
        self.arrived("f2p", "f2m")
        t = self.view(0, 0)
        t[...] = (
            t[...].astype(F32) + self.b["f2p"][...].astype(F32) + self.b["f2m"][...].astype(F32)
        ).astype(BF16)
        self.go("h", t.at[pl.ds(16, 16)], self.b["h"], "zh")

    def result(self):
        self.arrived("h")
        return self.view(0, 0)[0:16, :].astype(F32) + self.b["h"][...].astype(F32)

    def finish(self):
        for k in KEYS:
            if k != "c":
                self.made[k].wait_send()


def half_bufs(n, w):
    return [
        pltpu.VMEM((n, 4, 4, 32, w), BF16),
        pltpu.VMEM((n, 2, 2, 32, w), BF16),
        pltpu.VMEM((n, 2, 4, 32, w), BF16),
        pltpu.VMEM((n, 2, 16, w), BF16),
        pltpu.VMEM((n, 2, 32, w), BF16),
        pltpu.VMEM((n, 16, w), BF16),
    ]


def halves(n, to, refs, sems, rems, base):
    s, e1, e2, f1, f2, h = refs
    out = []
    for i in range(n):
        bufs = {
            "e1p": e1.at[i, 0],
            "e1m": e1.at[i, 1],
            "e2p": e2.at[i, 0],
            "e2m": e2.at[i, 1],
            "f1p": f1.at[i, 0],
            "f1m": f1.at[i, 1],
            "f2p": f2.at[i, 0],
            "f2m": f2.at[i, 1],
            "h": h.at[i],
        }
        out.append(Half(i % 2, to, s.at[i], bufs, sems.at[base + i], rems.at[base + i]))
    return out


def tiles(n, body):
    lax.fori_loop(0, n, lambda i, _: (body(i), 0)[1], 0)


def mult(i, n):
    return pl.multiple_of(i * n, n)


def flat(v):
    return v.reshape(-1, v.shape[-1])


def turned(perm, at, a_ref):
    for k in range(2):
        at[k][...] = nt(perm[k], a_ref[...]).astype(BF16)


def order_matrix(perm, place):
    y, zh, x, c = place
    k = lax.broadcasted_iota(jnp.int32, (1, D), 1)
    k16 = k >> 4
    crel = ((k16 & 1) - c) & 1
    xrel = (((k16 >> 1) & 3) - x) & 3
    zrel = (((k16 >> 3) & 1) - zh) & 1
    yrel = ((k16 >> 4) - y) & 3
    pos = (((crel * 4 + xrel) * 4 + yrel) * 2 + zrel) * 16 + (k & 15)

    for b in range(2):

        def step(t, b=b):
            r = lax.broadcasted_iota(jnp.int32, (64, D), 0) + (b * 512 + t * 64)
            perm[b, pl.ds(mult(t, 64), 64), :] = jnp.where(r == pos, 1.0, 0.0).astype(BF16)

        tiles(8, step)


def block_kernel(
    tok_in, cot_in, win_in, wout_in, wg_in, wu_in, wd_in, cw_in, g1_in, g2_in,
    bo, tg, gate_o, up_o, down_o, out_o, in_o, ng_o, fg_o, cg_o,
    wbuf, wd, win, wout, xv, cot, hv, p, bx, yv, u, da, db, dm, dsend, drecv, mrecv,
    dce, perm, xnt, cott, own, xr, br, rd, rdr, r1v, acc, vs, vx, vy, halo_p, halo_n,
    s_f, e1_f, e2_f, f1_f, f2_f, h_f, s_t, e1_t, e2_t, f1_t, f2_t, h_t,
    cw, g1, g2, lsem, rs_s, rs_r, ms, mr,
):
    s, sh, place, to = neighbours()
    mine = pl.ds(mult(sh, 512), 512)
    theirs = pl.ds(mult(1 - sh, 512), 512)
    loads = []

    def load(src, dst):
        copy = pltpu.make_async_copy(src, dst, lsem.at[len(loads)])
        copy.start()
        loads.append(copy)
        return copy

    made = []

    def go(src, dst, name):
        k = len(made)
        copy = send(src, dst, ms.at[k], mr.at[k], to[name])
        copy.start()
        made.append(copy)
        return copy

    l_tok = load(tok_in, xv.at[:, mine])
    l_win = [load(win_in.at[j], win.at[:, pl.ds(512 * j, 512)]) for j in range(3)]
    greet(to, ("z", "c", "xp", "xm", "x2", "yp", "ym", "y2", "zh", "nx", "pv"))
    parts = [pl.ds(0, 256), pl.ds(256, 256)]
    z_tok = [None, None]
    for r in (1, 0):
        z_tok[r] = go(tok_in.at[parts[r]], xv.at[parts[r], mine], "z")

    cw[0:3, :] = cw_in[...].astype(F32)
    g1[...] = g1_in[...].astype(F32).reshape(1, D)
    g2[...] = g2_in[...].astype(F32).reshape(1, D)
    l_wout = load(wout_in, wout)
    l_tok.wait()
    for l in l_win:
        l.wait()

    def project(r):

        def step(t):
            rows = pl.ds(pl.multiple_of(r * 256 + t * 32, 32), 32)
            xf = xv[rows, :].astype(F32)
            r1 = lax.rsqrt(jnp.mean(xf * xf, axis=-1, keepdims=True) + NORM_EPS)
            r1v[rows, :] = jnp.broadcast_to(r1, (32, 128))
            dm[rows, :] = (xf * r1 * g1[...]).astype(BF16)

        tiles(8, step)
        rows = parts[r]
        for n in range(2):
            c = 256 * n
            tb = nn(dm[rows, :], win[:, c : c + 256])
            tx = nn(dm[rows, :], win[:, 1024 + c : 1280 + c])
            p[rows, c : c + 256] = tb.astype(BF16)
            p[rows, 1024 + c : 1280 + c] = tx.astype(BF16)
            bx[pl.ds(8 + 256 * r, 256), c : c + 256] = tb * tx
            tc = nn(dm[rows, :], win[:, 512 + c : 768 + c])
            dce[rows, c : c + 256] = tc
            p[rows, 512 + c : 768 + c] = tc.astype(BF16)

    z_tok[1].wait_recv()
    l_cot = load(cot_in, cot.at[:, mine])
    l_wg = load(wg_in, wbuf.at[0])
    l_wu = load(wu_in, wbuf.at[1])
    l_wd = load(wd_in, wd)
    project(1)
    z_halo = go(bx.at[pl.ds(512, 8)], halo_p, "nx")
    z_tok[0].wait_recv()
    z_cot = go(cot_in, cot.at[:, mine], "z")
    project(0)
    z_halo.wait_recv()
    bx[0:8, :] = jnp.where(mod(s, 32) == 0, 0.0, halo_p[...])
    l_wout.wait()
    z_m = []
    for r in range(2):

        def step(t, r=r):
            base = r * 256 + t * 64
            w = bx[pl.ds(pl.multiple_of(base, 64), 72), :]
            conv = cw[0:1, :] * w[6:70] + cw[1:2, :] * w[7:71] + cw[2:3, :] * w[8:72]
            rows = pl.ds(pl.multiple_of(base, 64), 64)
            yv[rows, :] = (dce[rows, :] * conv).astype(BF16)

        tiles(4, step)
        rows = parts[r]
        for n in range(2):
            cols = pl.ds(512 * n, 512)
            dsend[rows, cols] = nn(yv[rows, :], wout[:, cols]).astype(BF16)
        z_m.append(go(dsend.at[rows], mrecv.at[rows], "z"))

    order_matrix(perm, place)
    turned(perm, [xnt.at[0], xnt.at[1]], dm)
    l_cot.wait()
    z_cot.wait_recv()
    cott = [cott.at[0], cott.at[1]]
    turned(perm, cott, cot)

    for l in (l_wg, l_wu, l_wd):
        l.wait()
    z_dhn = []
    for r in range(2):
        z_m[r].wait_recv()

        def step(t, r=r):
            rows = pl.ds(pl.multiple_of(r * 256 + t * 32, 32), 32)
            hf = xv[rows, :].astype(F32) + dsend[rows, :].astype(F32) + mrecv[rows, :].astype(F32)
            hv[rows, :] = hf.astype(BF16)
            r2 = lax.rsqrt(jnp.mean(hf * hf, axis=-1, keepdims=True) + NORM_EPS)
            dm[rows, :] = (hf * r2 * g2[...]).astype(BF16)

        tiles(8, step)
        rows = parts[r]
        for n in range(9):
            cols = pl.ds(256 * n, 256)
            a = nn(dm[rows, :], flat(wbuf[0, :, :, :, :, cols]))
            b = nn(dm[rows, :], flat(wbuf[1, :, :, :, :, cols]))
            du = nt(cot[rows, :], wd[cols, :])
            sig = jax.nn.sigmoid(a)
            silu = a * sig
            u[rows, cols] = (silu * b).astype(BF16)
            db[rows, cols] = (du * silu).astype(BF16)
            da[rows, cols] = (du * b * (sig + silu * (1.0 - sig))).astype(BF16)
        z_m[r].wait_send()
        for n in range(2):
            t = nt(da[rows, :], flat(wbuf[0, n])) + nt(db[rows, :], flat(wbuf[1, n]))
            dsend[rows, pl.ds(512 * n, 512)] = t.astype(BF16)
        z_dhn.append(go(dsend.at[rows], drecv.at[rows], "z"))

    hnt = [mrecv.at[:, pl.ds(512 * k, 512)] for k in range(2)]
    dmt = cott
    dp = wbuf.at[1, 1]
    xs = wbuf.at[1, 1, :, :, :, pl.ds(1536, HALF)]
    rds = wbuf.at[1, 1, :, :, :, pl.ds(2048, 128)]
    turned(perm, hnt, dm)
    ffn = halves(6, to, (s_f, e1_f, e2_f, f1_f, f2_f, h_f), rs_s, rs_r, 0)
    tail = halves(2, to, (s_t, e1_t, e2_t, f1_t, f2_t, h_t), rs_s, rs_r, 6)
    ffn_parts = [(hnt, da), (hnt, db), (cott, u)]
    slots = [wbuf.at[0, 0], wbuf.at[0, 1], wbuf.at[1, 0]]

    def ffn_send(k):
        at, b = ffn_parts[k]
        for n in range(3):
            cols = pl.ds(768 * n, 768)
            t = nn(at[1][...], b[:, cols])
            slots[k][:, :, :, cols] = t.astype(BF16).reshape(4, 4, 32, 768)
            if n == 1:
                ffn[2 * k].core(slots[k].at[:, :, :, pl.ds(0, WF)])
        ffn[2 * k + 1].core(slots[k].at[:, :, :, pl.ds(WF, WF)])

    def into(ref, cols, t):
        ref[:, :, :, cols] = (
            t.reshape(4, 4, 32, t.shape[-1]) + ref[:, :, :, cols].astype(F32)
        ).astype(BF16)

    def ffn_keep(k):
        at, b = ffn_parts[k]
        lo, hi = s_f.at[2 * k], s_f.at[2 * k + 1]
        ffn[2 * k].arrived("c")
        t = nn(at[0][...], b[:, 0:768])
        into(lo, pl.ds(0, 768), t)
        ffn[2 * k + 1].arrived("c")
        t = nn(at[0][...], b[:, 768:1536])
        into(lo, pl.ds(768, 384), t[:, 0:384])
        ffn[2 * k].e1()
        into(hi, pl.ds(0, 384), t[:, 384:768])
        t = nn(at[0][...], b[:, 1536:2304])
        into(hi, pl.ds(384, 768), t)
        ffn[2 * k + 1].e1()

    ffn_send(0)
    ffn_send(1)
    ffn_send(2)
    ffn_keep(0)
    ffn_keep(1)
    ffn_keep(2)
    for i in range(2):
        ffn[i].e2()

    acc[...] = jnp.zeros_like(acc)

    def mixer(r):

        def step(t):
            rows = pl.ds(pl.multiple_of(r * 256 + t * 32, 32), 32)
            hf = hv[rows, :].astype(F32)
            r2 = lax.rsqrt(jnp.mean(hf * hf, axis=-1, keepdims=True) + NORM_EPS)
            dhn = dsend[rows, :].astype(F32) + drecv[rows, :].astype(F32)
            acc[0:8, :] += (dhn * hf * r2).reshape(4, 8, D).sum(axis=0)
            scaled = dhn * g2[...]
            dot = jnp.mean(scaled * hf, axis=-1, keepdims=True)
            d = cot[rows, :].astype(F32) + r2 * scaled - hf * (r2 * r2 * r2 * dot)
            dm[rows, :] = d.astype(BF16)
            tg[rows, :] = jnp.where(sh == 0, d[:, 0:512], d[:, 512:1024])

        tiles(8, step)
        rows = parts[r]
        dy = nt(dm[rows, :], wout[...])
        own[rows, :] = dy.astype(BF16)
        dce[rows, :] = dy * p[rows, 512:1024].astype(F32)

    xs[...] = nn(u[...], wd[:, theirs]).astype(BF16).reshape(4, 4, 32, HALF)
    z_dhn[0].wait_recv()
    mixer(0)
    back = go(dce.at[pl.ds(0, 8)], halo_n, "pv")
    for i in range(2, 4):
        ffn[i].e2()
    z_dhn[1].wait_recv()
    z_out = go(xs, br, "z")
    mixer(1)
    back.wait_recv()
    back.wait_send()
    dce[512:520, :] = jnp.where(mod(s, 32) == 31, 0.0, halo_n[...])

    def dstep(t):
        rows = pl.ds(mult(t, 64), 64)
        ext = pl.ds(mult(t, 64), 72)
        dc = dce[ext, :]
        w = bx[ext, :]
        d0 = dc[0:64]
        b2, b1, b0 = w[6:70], w[7:71], w[8:72]
        acc[8:16, 0:512] += (d0 * b2).reshape(8, 8, 512).sum(axis=0)
        acc[16:24, 0:512] += (d0 * b1).reshape(8, 8, 512).sum(axis=0)
        acc[24:32, 0:512] += (d0 * b0).reshape(8, 8, 512).sum(axis=0)
        conv = cw[0:1, :] * b2 + cw[1:2, :] * b1 + cw[2:3, :] * b0
        dbx = cw[2:3, :] * d0 + cw[1:2, :] * dc[1:65] + cw[0:1, :] * dc[2:66]
        at = (t // 2, pl.ds(mod(t, 2) * 2, 2))

        def put(col, v):
            dp[at[0], at[1], :, col : col + 512] = v.astype(BF16).reshape(2, 32, 512)

        put(0, dbx * p[rows, 1024:1536].astype(F32))
        put(512, own[rows, :].astype(F32) * conv)
        put(1024, dbx * p[rows, 0:512].astype(F32))

    tiles(8, dstep)

    rd[...] = jnp.zeros_like(rd)

    def dxn(half, dst):
        for n in range(2):
            wr = pl.ds(pl.multiple_of(half * 512 + n * 256, 256), 256)
            for r, rows in enumerate(parts):
                t = nt(flat(dp[2 * r : 2 * r + 2, :, :, 0:1536]), win[wr, :])
                tx = t * xv[rows, wr].astype(F32)
                rd[rows, :] += jnp.broadcast_to(
                    jnp.sum(tx * g1[:, wr], axis=-1, keepdims=True), (256, 128)
                )
                acc[32:40, wr] += (tx * r1v[rows, 0:1]).reshape(32, 8, 256).sum(axis=0)
                dst[rows, pl.ds(256 * n, 256)] = t.astype(dst.dtype)

    dxn(1 - sh, mrecv.at[:, pl.ds(0, 512)])
    for i in range(4, 6):
        ffn[i].e2()
    dxn(sh, dce)
    hi = rd[...].astype(BF16)
    lo = (rd[...] - hi.astype(F32)).astype(BF16)
    lane = lax.broadcasted_iota(jnp.int32, (ROWS, 128), 1)
    both = jnp.where(lane < 64, hi.astype(F32), lo.astype(F32))
    rds[...] = both.astype(BF16).reshape(4, 4, 32, 128)
    z_rd = go(rds, rdr, "z")

    row = lax.broadcasted_iota(jnp.int32, (8, D), 0)

    def total(lo_):
        t = jnp.sum(acc[lo_ : lo_ + 8, :], axis=0, keepdims=True)
        return jnp.broadcast_to(t, (8, D))

    v = jnp.where(row == 0, total(32), 0.0)
    v = jnp.where(row == 1, 0.5 * total(0), v)
    v = jnp.where(row == 2, total(8), v)
    v = jnp.where(row == 3, total(16), v)
    v = jnp.where(row == 4, total(24), v)
    vs[0] = v
    v_z = go(vs.at[0], vs.at[5], "z")
    z_dxn = go(mrecv.at[:, pl.ds(0, 512)], xr, "z")

    turned(perm, dmt, dm)

    def tail_gemm(i, k, store):
        store(pl.ds(0, 256), nn(dmt[k][...], yv[:, 256 * i : 256 * i + 256]))
        store(pl.ds(256, 768), nn(xnt[k], flat(dp[:, :, :, 768 * i : 768 * i + 768])))

    for i in range(2):
        ffn[i].made["c"].wait_send()

        def store(cols, t, i=i):
            here = pl.ds(i * WF + cols.start, cols.size)
            slots[0][:, :, :, here] = t.astype(BF16).reshape(4, 4, 32, cols.size)

        tail_gemm(i, 1, store)
        tail[i].core(slots[0].at[:, :, :, pl.ds(i * WF, WT)])

    def tail_keep(i):
        tail[i].arrived("c")
        tail_gemm(i, 0, lambda cols, t: into(s_t.at[i], cols, t))
        tail[i].e1()

    def each(lo_, hi_, name):
        for i in range(lo_, hi_):
            getattr(ffn[i], name)()

    each(0, 2, "f1")
    tail_keep(0)
    tail_keep(1)
    each(2, 4, "f1")
    v_z.wait_recv()
    vs[1] = vs[0] + jnp.where(row < 2, vs[5], 0.0)
    v_c = go(vs.at[1], vs.at[6], "c")
    each(0, 2, "f2")
    each(4, 6, "f1")
    for i in range(2):
        tail[i].e2()
    v_c.wait_recv()
    vs[2] = vs[1] + vs[6]
    y, zh, x, c = place
    vx[x] = vs[2]
    v_x = [go(vs.at[2], vx.at[x], n) for n in ("xp", "xm", "x2")]
    each(2, 4, "f2")

    z_dxn.wait_recv()
    z_rd.wait_recv()

    def tstep(t):
        rows = pl.ds(mult(t, 64), 64)
        r1 = r1v[rows, 0:1]
        d = dce[rows, :] + xr[rows, :].astype(F32)
        q = flat(rdr[t // 2, pl.ds(mod(t, 2) * 2, 2)]).astype(F32)
        mean = (rd[rows, 0:1] + q[:, 0:1] + q[:, 64:65]) * (1.0 / D)
        xo = xv[rows, mine].astype(F32)
        tg[rows, :] += r1 * (d * g1[:, mine]) - xo * (r1 * r1 * r1 * mean)

    tiles(8, tstep)
    each(4, 6, "f2")
    for i in range(2):
        tail[i].f1()
    for w in v_x:
        w.wait_recv()
    vs[3] = (vx[0] + vx[1]) + (vx[2] + vx[3])
    vy[y] = vs[3]
    v_y = [go(vs.at[3], vy.at[y], n) for n in ("yp", "ym", "y2")]
    each(0, 4, "hop")
    bo[...] = (nn(u[...], wd[:, mine]) + hv[:, mine].astype(F32)).astype(BF16)
    for i in range(2):
        tail[i].f2()
    each(4, 6, "hop")
    for w in v_y:
        w.wait_recv()
    vs[4] = (vy[0] + vy[1]) + (vy[2] + vy[3])
    v_h = go(vs.at[4], vs.at[7], "zh")
    for i in range(2):
        tail[i].hop()
    for i, o in enumerate((gate_o, up_o, down_o)):
        o[:, 0:WF] = ffn[2 * i].result()
        o[:, WF : 2 * WF] = ffn[2 * i + 1].result()
    z_out.wait_recv()
    bo[...] = (bo[...].astype(F32) + flat(br[...]).astype(F32)).astype(BF16)
    v_h.wait_recv()
    v = vs[4] + vs[7]
    ng_o[...] = v[0:1, :]
    fg_o[...] = v[1:2, :]
    cg_o[...] = v[2:5, 0:512]
    for i in range(2):
        t = tail[i].result()
        out_o[:, 256 * i : 256 * i + 256] = t[:, 0:256]
        for j in range(6):
            n = 768 * i + 128 * j
            in_o[n // 512, :, n % 512 : n % 512 + 128] = t[:, 256 + 128 * j : 384 + 128 * j]
    for q in made:
        if all(q is not d for d in (*z_m, back)):
            q.wait_send()
    for q in ffn + tail:
        q.finish()
    for q in ffn[2:] + tail:
        q.made["c"].wait_send()


def block(*args):
    hbm = pl.BlockSpec(memory_space=pl.ANY)
    vm = pl.BlockSpec(memory_space=pltpu.VMEM)
    sds = jax.ShapeDtypeStruct
    scratch = [
        pltpu.VMEM((2, 2, 4, 4, 32, FFH), BF16),
        pltpu.VMEM((FFH, D), BF16),
        pltpu.VMEM((D, 3 * HALF), BF16),
        pltpu.VMEM((HALF, D), BF16),
        pltpu.VMEM((ROWS, D), BF16),
        pltpu.VMEM((ROWS, D), BF16),
        pltpu.VMEM((ROWS, D), BF16),
        pltpu.VMEM((ROWS, 3 * HALF), BF16),
        pltpu.VMEM((ROWS + 8, HALF), F32),
        pltpu.VMEM((ROWS, HALF), BF16),
        pltpu.VMEM((ROWS, FFH), BF16),
        pltpu.VMEM((ROWS, FFH), BF16),
        pltpu.VMEM((ROWS, FFH), BF16),
        pltpu.VMEM((ROWS, D), BF16),
        pltpu.VMEM((ROWS, D), BF16),
        pltpu.VMEM((ROWS, D), BF16),
        pltpu.VMEM((ROWS, D), BF16),
        pltpu.VMEM((ROWS + 8, HALF), F32),
        pltpu.VMEM((2, HALF, D), BF16),
        pltpu.VMEM((2, HALF, ROWS), BF16),
        pltpu.VMEM((2, HALF, ROWS), BF16),
        pltpu.VMEM((ROWS, HALF), BF16),
        pltpu.VMEM((ROWS, HALF), BF16),
        pltpu.VMEM((4, 4, 32, HALF), BF16),
        pltpu.VMEM((ROWS, 128), F32),
        pltpu.VMEM((4, 4, 32, 128), BF16),
        pltpu.VMEM((ROWS, 128), F32),
        pltpu.VMEM((40, D), F32),
        pltpu.VMEM((8, 8, D), F32),
        pltpu.VMEM((4, 8, D), F32),
        pltpu.VMEM((4, 8, D), F32),
        pltpu.VMEM((8, HALF), F32),
        pltpu.VMEM((8, HALF), F32),
        *half_bufs(6, WF),
        *half_bufs(2, WT),
        pltpu.VMEM((8, HALF), F32),
        pltpu.VMEM((1, D), F32),
        pltpu.VMEM((1, D), F32),
        pltpu.SemaphoreType.DMA((16,)),
        pltpu.SemaphoreType.DMA((8, len(KEYS))),
        pltpu.SemaphoreType.DMA((8, len(KEYS))),
        pltpu.SemaphoreType.DMA((24,)),
        pltpu.SemaphoreType.DMA((24,)),
    ]
    return pl.pallas_call(
        block_kernel,
        out_shape=(
            sds((ROWS, HALF), BF16),
            sds((ROWS, HALF), F32),
            sds((16, FFH), F32),
            sds((16, FFH), F32),
            sds((16, FFH), F32),
            sds((16, HALF), F32),
            sds((3, 16, HALF), F32),
            sds((1, D), F32),
            sds((1, D), F32),
            sds((3, HALF), F32),
        ),
        in_specs=[hbm] * 7 + [vm] * 3,
        out_specs=(vm,) * 10,
        scratch_shapes=scratch,
        compiler_params=pltpu.CompilerParams(
            collective_id=1, has_side_effects=True, vmem_limit_bytes=VMEM_LIMIT
        ),
        cost_estimate=pl.CostEstimate(
            flops=32_000_000_000, bytes_accessed=24_000_000, transcendentals=0
        ),
        name="block",
    )(*args)


def settle_kernel(*refs):
    n = len(refs) // 2
    for i in range(n):
        refs[n + i][...] = refs[i][...]


def settle(arrays):
    n = len(arrays)
    vm = pl.BlockSpec(memory_space=pltpu.VMEM)
    return pl.pallas_call(
        settle_kernel,
        out_shape=tuple(jax.ShapeDtypeStruct(a.shape, a.dtype) for a in arrays),
        in_specs=[vm] * n,
        out_specs=(vm,) * n,
        compiler_params=pltpu.CompilerParams(vmem_limit_bytes=VMEM_LIMIT),
        name="settle",
    )(*arrays)


def body(
    tokens, norm_gain, in_weight, conv_weight, out_weight, ffn_gain, gate_weight, up_weight,
    down_weight, cotangent,
):
    bo, tg, gate_g, up_g, down_g, out_g, in_g, ng, fg, cg = settle(
        block(
            tokens,
            cotangent,
            in_weight.transpose(1, 0, 2),
            out_weight,
            gate_weight.reshape(2, 4, 4, 32, FFH),
            up_weight.reshape(2, 4, 4, 32, FFH),
            down_weight,
            conv_weight,
            norm_gain,
            ffn_gain,
        )
    )
    return (
        bo,
        tg,
        ng.reshape(D),
        in_g.transpose(1, 0, 2),
        cg,
        out_g.T,
        fg.reshape(D),
        gate_g,
        up_g,
        down_g.T,
    )


def solution(mesh):
    return jax.shard_map(
        body,
        mesh=mesh,
        in_specs=(
            P("seq", "shard"),
            P(),
            P(None, None, "shard"),
            P(None, "shard"),
            P("shard", None),
            P(),
            P(None, "shard"),
            P(None, "shard"),
            P("shard", None),
            P("seq", "shard"),
        ),
        out_specs=(
            P("seq", "shard"),
            P("seq", "shard"),
            P(),
            P("seq", None, "shard"),
            P(None, "shard"),
            P("shard", "seq"),
            P(),
            P("seq", "shard"),
            P("seq", "shard"),
            P("shard", "seq"),
        ),
        check_vma=False,
    )
```
